256 devices in a mesh: band: 32 (over x_hi, z, core), fft: 8 (over y, x_lo).
Axes of the slice: x: 4 (x_hi: 2, x_lo: 2; x = x_hi * 2 + x_lo), y: 4, z: 8, core: 2. Of those that a mesh axis runs over, the one named last changes fastest.
Arguments:
- coefficients: float32 [32, 675840], P(None, ('band', 'fft')), may hold values from -0.01171875 to 0.01171875
- owned_sticks: int32 [8, 704], P('fft'), may hold values from -1 to 351, as said below
- stick_counts: int32 [8, 352], P('fft'), may hold values from 61 to 119, as said below
- stick_columns: int32 [8, 352], P('fft'), may hold values from 0 to 1799, as said below
- band_order: int32 [32], replicated, may hold values from 0 to 31, each once
Outputs:
- exchange_field: float32 [32, 120, 14400], P('band', 'fft')
The draws below stay inside these ranges and needn't reach their ends.
Inputs may be any that keep to these rules, and one draw needn't show every extreme that they name: `owned_sticks`: in each row every stick number appears exactly once; each block of 22 entries lists the sticks of one owner along band, -1 marking an empty slot; in each row one owner fills all 22 slots. `stick_counts`: Odd; each row has a stick with 120 - 1 G-vectors. `stick_columns`: the sticks of one row lie in distinct columns. `band_order`: each band appears once.
All inputs are finite; a program needn't handle non-finite values.
Results may differ from the reference program's by a relative error of at most 0.0003.
Values sent between devices are 32-bit elements; how exact they have to be, the bound alone decides.
A program may use at most 128 MiB of HBM per device.

```python
import math
import jax
import jax.numpy as jnp
from jax import lax

NX = 120
NY = 120
NZ = 120
BANDS_DEV = 1
STOPS = 1
OWN_MEAN = 11
NB = 32
STICK_F = 352
OWN_CAP = 22
COLUMNS = 1800
N_BAND = 32
N_FFT = 8


def ownership_row(key):
    key_share, key_swing, key_rank, key_slot = jax.random.split(key, 4)
    extra_share = jax.random.randint(key_share, (1,), 0, OWN_MEAN + 1).astype(jnp.int32)
    pair_count = (N_BAND - 3) // 2
    swing_size = jax.random.randint(key_swing, (pair_count,), -OWN_MEAN, OWN_MEAN + 1).astype(jnp.int32)
    paired = jnp.stack([OWN_MEAN + swing_size, OWN_MEAN - swing_size], axis=1).reshape(-1)
    leftover = jnp.full((N_BAND - 3 - 2 * pair_count,), OWN_MEAN, jnp.int32)
    ranked = jnp.concatenate([jnp.full((1,), OWN_CAP, jnp.int32), extra_share, OWN_MEAN - extra_share, paired, leftover]).astype(jnp.int32)
    owner_rank = jax.random.permutation(key_rank, N_BAND)
    owned_count = jnp.zeros((N_BAND,), jnp.int32).at[owner_rank].set(ranked)
    starts = jnp.cumsum(owned_count) - owned_count
    shuffled = jax.random.permutation(key_slot, STICK_F).astype(jnp.int32)
    position = jnp.arange(OWN_CAP, dtype=jnp.int32)
    wanted = starts[:, None] + position[None, :]
    in_range = position[None, :] < owned_count[:, None]
    picked = shuffled[jnp.clip(wanted, 0, STICK_F - 1)]
    return jnp.where(in_range, picked, -1).reshape(-1).astype(jnp.int32)


def draw_owned_sticks(key, part):
    key = jax.random.fold_in(key, 3)
    return jax.vmap(ownership_row)(jax.random.split(key, N_FFT))


def draw_stick_counts(key, part):
    key = jax.random.fold_in(key, 5)
    key_half, key_top = jax.random.split(key)
    half_len = jax.random.randint(key_half, (N_FFT, STICK_F), NZ // 4, NZ // 2).astype(jnp.int32)
    longest = jax.random.randint(key_top, (N_FFT,), 0, STICK_F).astype(jnp.int32)
    row_ids = jnp.arange(N_FFT, dtype=jnp.int32)
    half_len = half_len.at[row_ids, longest].set(NZ // 2 - 1)
    half_len = half_len.at[row_ids, (longest + 1) % STICK_F].set(NZ // 4)
    return (2 * half_len + 1).astype(jnp.int32)


def column_row(key):
    key_pick, key_mix = jax.random.split(key)
    middle_cols = (jax.random.permutation(key_pick, COLUMNS - 2) + 1)[:STICK_F - 2]
    chosen = jnp.concatenate([jnp.array([0, COLUMNS - 1], jnp.int32), middle_cols.astype(jnp.int32)])
    return jax.random.permutation(key_mix, chosen).astype(jnp.int32)


def draw_stick_columns(key, part):
    key = jax.random.fold_in(key, 7)
    return jax.vmap(column_row)(jax.random.split(key, N_FFT))


def level_of(rng, dims, cuts, low, high):
    gain = 1.0
    for dim, shards_of in cuts:
        heights = jax.random.uniform(jax.random.fold_in(jax.random.fold_in(rng, 6), dim), (shards_of,), jnp.float32, low / len(cuts), high / len(cuts))
        gain = gain * jnp.repeat(jnp.exp(heights), dims[dim] // shards_of).reshape((-1,) + (1,) * (len(dims) - 1 - dim))
    return gain


def bell_draw(key, extent, scale, reach, pieces=(), held_as=jnp.bfloat16):
    factor_of = level_of(key, extent, pieces, -0.22, 0.18) if pieces else 1.0
    drawn = jax.random.normal(key, extent, jnp.float32) * scale * factor_of
    return jnp.minimum(jnp.maximum(drawn, -reach), reach).astype(held_as)


def setup_inputs(seed: int = 0) -> dict:
    seeds = jax.random.split(jax.random.key(seed), 6)
    return {
        "coefficients": bell_draw(seeds[0], (NB, N_BAND * N_FFT * OWN_CAP * NZ), (STICK_F * N_FFT * 3 * NZ // 4) ** -0.5, 0.01171875, ((1, 256),), jnp.float32),
        "owned_sticks": draw_owned_sticks(jax.random.fold_in(seeds[5], 71), 0),
        "stick_counts": draw_stick_counts(jax.random.fold_in(seeds[5], 71), 0),
        "stick_columns": draw_stick_columns(jax.random.fold_in(seeds[5], 71), 0),
        "band_order": jax.random.permutation(seeds[4], NB).astype(jnp.int32),
    }


COULOMB = 0.25
EXCHANGE_FRACTION = 0.25

def centered(position, length):
    return jnp.where(position > length // 2, position - length, position)

def hartley(field_in, axis_id):
    spectrum = jnp.fft.fft(field_in, axis=axis_id)
    return jnp.real(spectrum) - jnp.imag(spectrum)

def hartley_all(field_in):
    return hartley(hartley(hartley(field_in, 0), 1), 2)

def coulomb_table():
    z_freq = centered(jnp.arange(NZ, dtype=jnp.int32), NZ)
    x_freq = centered(jnp.arange(NX, dtype=jnp.int32), NX)
    y_freq = centered(jnp.arange(NY, dtype=jnp.int32), NY)
    square = (z_freq * z_freq)[:, None, None] + (x_freq * x_freq)[None, :, None] + (y_freq * y_freq)[None, None, :]
    volume = NX * NY * NZ
    scale_factor = COULOMB * math.sqrt(volume) / volume
    return jnp.where(square > 0, scale_factor / jnp.maximum(square.astype(jnp.float32), 1.0), 0.0).astype(jnp.float32)

def reference(coefficients, owned_sticks, stick_counts, stick_columns, band_order):
    columns_dev = NX * NY // N_FFT
    slot_rows = coefficients.reshape(NB, N_BAND, N_FFT, OWN_CAP, NZ).transpose(0, 2, 1, 3, 4)
    slot_rows = slot_rows.reshape(NB, N_FFT, N_BAND * OWN_CAP, NZ)
    owners = owned_sticks.reshape(N_FFT, N_BAND * OWN_CAP)
    safe_ids = jnp.clip(owners, 0, STICK_F - 1).astype(jnp.int32)
    counts_of = jnp.take_along_axis(stick_counts, safe_ids, axis=1)
    counts_of = jnp.where(owners >= 0, counts_of, 0)
    column_of = jnp.take_along_axis(stick_columns, safe_ids, axis=1)
    column_of = column_of + (jnp.arange(N_FFT, dtype=jnp.int32) * columns_dev)[:, None]
    column_of = jnp.where(owners >= 0, column_of, NX * NY).astype(jnp.int32)
    z_freq = centered(jnp.arange(NZ, dtype=jnp.int32), NZ)
    keep_mask = jnp.abs(z_freq)[None, None, :] <= ((counts_of - 1) // 2)[:, :, None]
    kept_rows = jnp.where(keep_mask[None], slot_rows, 0.0)
    spectrum = jnp.zeros((NB, NX * NY, NZ), jnp.float32)
    spectrum = spectrum.at[:, column_of.reshape(-1), :].set(kept_rows.reshape(NB, N_FFT * N_BAND * OWN_CAP, NZ), mode='drop')

    def make_orbital(band_id):
        cube_view = spectrum[band_id].reshape(NX, NY, NZ).transpose(2, 0, 1)
        return hartley_all(cube_view)
    orbitals = lax.map(make_orbital, band_order)
    kernel_table = coulomb_table()

    def one_band(slot_index):
        group_id = slot_index // BANDS_DEV
        left_band = orbitals[slot_index]
        running_sum = jnp.zeros((NZ, NX, NY), jnp.float32)
        for offset in range(-STOPS, STOPS + 1):
            other_group = (group_id + offset) % N_BAND
            for slot_idx in range(BANDS_DEV):
                right_band = orbitals[other_group * BANDS_DEV + slot_idx]
                field_pot = hartley_all(kernel_table * hartley_all(left_band * right_band))
                running_sum = running_sum + field_pot * right_band
        return (-EXCHANGE_FRACTION * running_sum).reshape(NZ, NX * NY)
    return lax.map(one_band, jnp.arange(NB, dtype=jnp.int32))
```

```python
import math

import jax
import jax.numpy as jnp
import ml_dtypes
import numpy as np
from jax import lax
from jax.experimental import pallas as pl
from jax.experimental.pallas import tpu as pltpu
from jax.sharding import PartitionSpec as P

N = 120
NF = 8
NBAND = 32
ZL = N // NF
ZP = 16
CAP = 22
CAPP = 24
STICKS = 352
STP = 384
L = 128
BLK = ZL * ZP
COULOMB = 0.25
EXCHANGE_FRACTION = 0.25
F32 = jnp.float32
BF16 = jnp.bfloat16


def cas_parts():
    k = np.arange(N)
    angle = (k[:, None] * k[None, :] % N) * (2.0 * math.pi / N)
    full = np.cos(angle) + np.sin(angle)
    zpad = (k // ZL) * ZP + k % ZL

    def parts(a):
        hi = a.astype(ml_dtypes.bfloat16)
        lo = (a - hi.astype(np.float64)).astype(ml_dtypes.bfloat16)
        return hi, lo

    def place(rows, cols):
        out = np.zeros((L, L))
        out[np.ix_(rows, cols)] = full
        return out

    def right(a):
        hi, lo = parts(a)
        row = np.concatenate([hi, lo], axis=1)
        return np.concatenate([row, row], axis=0)

    def left(a):
        hi, lo = parts(a)
        return np.concatenate([hi, lo], axis=1)

    plain = place(k, k)
    return (
        right(plain),
        right(place(k, zpad)),
        left(plain),
        left(place(k, zpad)),
        left(place(zpad, k)),
    )


def halves(x):
    hi = x.astype(BF16)
    lo = (x - hi.astype(F32)).astype(BF16)
    return jnp.concatenate([hi, lo], axis=1)


def fold(r):
    return r[:, :L] + r[:, L:]


def dot(a, b):
    return jnp.dot(a, b, preferred_element_type=F32)


def right_mul(x, table):
    return fold(dot(halves(x), table))


def left_mul(table, x):
    cat = halves(x)
    return fold(dot(table, jnp.concatenate([cat, cat], axis=0)))


def kernel(
    coef, owned, counts, cols, order, hr, hrz, lx, lz1, lz2, out,
    stage, stage3, send1, recv1, sel, keep, owned_p, cols_p, at_send, at_recv, phi, tb, tb2,
    coul, send_f, recv_f, send_b, recv_b, send_v, recv_v, acc,
    s1, r1, s2, r2, sf, rf, sb, rb, sv, rv,
):
    band = lax.axis_index("band")
    fft = lax.axis_index("fft")
    nxt = lax.rem(band + 1, NBAND)
    prv = lax.rem(band + NBAND - 1, NBAND)

    def copy(src, dst, ssem, rsem, b, f):
        return pltpu.make_async_remote_copy(
            src_ref=src, dst_ref=dst, send_sem=ssem, recv_sem=rsem,
            device_id=(b, f), device_id_type=pl.DeviceIdType.MESH,
        )

    barrier = pltpu.get_barrier_semaphore()

    def hello_band(d, c):
        pl.semaphore_signal(
            barrier, inc=1, device_id=(lax.rem(band + d, NBAND), fft),
            device_id_type=pl.DeviceIdType.MESH)
        return c

    lax.fori_loop(1, NBAND, hello_band, 0)

    def hello_fft(d, c):
        f = lax.rem(fft + d, NF)
        pl.semaphore_signal(
            barrier, inc=1, device_id=(band, f), device_id_type=pl.DeviceIdType.MESH)
        pl.semaphore_signal(
            barrier, inc=1, device_id=(nxt, f), device_id_type=pl.DeviceIdType.MESH)
        return c

    lax.fori_loop(1, NF, hello_fft, 0)

    stage[...] = jnp.zeros(stage.shape, F32)
    for q in range(CAP):
        stage[pl.ds(q, NBAND, stride=CAPP), pl.ds(0, N)] = coef[:, N * q:N * q + N]

    stage3[...] = stage[...].reshape(NBAND, CAPP, L)

    def reorder(j, c):
        send1[j] = stage3[order[j]]
        return c

    lax.fori_loop(0, NBAND, reorder, 0)

    pl.semaphore_wait(barrier, NBAND - 1 + 2 * (NF - 1))

    def go1(d, c):
        b = lax.rem(band + d, NBAND)
        copy(send1.at[b], recv1.at[band], s1.at[b], r1.at[band], b, fft).start()
        return c

    lax.fori_loop(1, NBAND, go1, 0)
    recv1[band] = send1[band]

    tb[...] = jnp.zeros(tb.shape, F32)
    tb2[...] = jnp.zeros(tb2.shape, F32)
    owned_p[...] = jnp.full(owned_p.shape, -1, jnp.int32)
    for o in range(NBAND):
        owned_p[:, CAPP * o:CAPP * o + CAP] = owned[:, CAP * o:CAP * o + CAP]
    rows = lax.broadcasted_iota(jnp.int32, (STICKS, NBAND * CAPP), 0)
    sel[...] = jnp.where(rows == owned_p[...], 1.0, 0.0).astype(BF16)
    cols_p[...] = jnp.full(cols_p.shape, -1.0, F32)
    cols_p[0:1, 0:STICKS] = cols[...].astype(F32)
    cols_p[1:2, 0:STICKS] = counts[...].astype(F32)
    count_b = jnp.transpose(jnp.broadcast_to(cols_p[1:2, :], (L, STP)))[:STICKS]
    kz = lax.broadcasted_iota(jnp.int32, (STICKS, L), 1)
    need = (2 * jnp.minimum(kz, N - kz) + 1).astype(F32)
    keep[...] = jnp.where((kz < N) & (need <= count_b), 1.0, 0.0)
    scale = -EXCHANGE_FRACTION * COULOMB * math.sqrt(N ** 3) / N ** 3
    r0 = lax.broadcasted_iota(jnp.int32, (L, L), 0)
    r1_ = lax.broadcasted_iota(jnp.int32, (L, L), 1)
    mz = jnp.minimum(r0, N - r0)
    my = jnp.minimum(r1_, N - r1_)
    plane = mz * mz + my * my

    def coulomb(x, c):
        kx = fft * ZL + x
        mx = jnp.minimum(kx, N - kx)
        q = (plane + mx * mx).astype(F32)
        coul[x] = jnp.where(q > 0.0, scale / jnp.maximum(q, 1.0), 0.0)
        return c

    lax.fori_loop(0, ZL, coulomb, 0)

    def got1(d, c):
        b = lax.rem(band + d, NBAND)
        copy(send1.at[b], recv1.at[b], s1.at[b], r1.at[b], b, fft).wait_recv()
        return c

    lax.fori_loop(1, NBAND, got1, 0)

    arrived = halves(recv1[...].reshape(NBAND * CAPP, L))
    picked = dot(sel[...], arrived)
    kept = keep[...] > 0.0
    hi = jnp.where(kept, picked[:, :L], 0.0).astype(BF16)
    lo = jnp.where(kept, picked[:, L:], 0.0).astype(BF16)
    along = fold(dot(jnp.concatenate([hi, lo], axis=1), hrz[...]))
    along = jnp.concatenate([along, jnp.zeros((STP - STICKS, L), F32)], axis=0)
    flipped = jnp.transpose(along)
    for f in range(NF):
        at_send[f] = flipped[f * ZP:(f + 1) * ZP]
        at_send[f, ZP - 1:ZP, :] = cols_p[0:1, :]

    def go2(d, c):
        f = lax.rem(fft + d, NF)
        copy(at_send.at[f], at_recv.at[0, fft], s2.at[0, f], r2.at[0, fft], band, f).start()
        return c

    def go2n(d, c):
        f = lax.rem(fft + d, NF)
        copy(at_send.at[f], at_recv.at[1, fft], s2.at[1, f], r2.at[1, fft], prv, f).start()
        return c

    lax.fori_loop(1, NF, go2, 0)
    lax.fori_loop(0, NF, go2n, 0)
    at_recv[0, fft] = at_send[fft]

    def got2(which, f):
        copy(at_send.at[f], at_recv.at[which, f], s2.at[which, f], r2.at[which, f],
             nxt, f).wait_recv()

    lax.fori_loop(1, NF, lambda d, c: (got2(0, lax.rem(fft + d, NF)), c)[1], 0)
    lax.fori_loop(0, NF, lambda d, c: (got2(1, d), c)[1], 0)

    srow = lax.broadcasted_iota(jnp.int32, (ZP, STP), 0)
    kyrow = lax.broadcasted_iota(jnp.int32, (L, STP), 0).astype(F32)

    def orbital(which):
        def spread(f, c):
            blk = at_recv[which, f]
            col = blk[ZP - 1:ZP, :]
            kx = jnp.floor((col + 0.5) * (1.0 / N))
            ky = col - N * kx
            a = jnp.where(srow < ZL, blk, 0.0)
            hot = jnp.where(kyrow == ky, 1.0, 0.0).astype(BF16)
            a_hi = a.astype(BF16).astype(F32)
            a_lo = a - a_hi
            his, los = [], []
            for x in range(ZL):
                hit = kx == x
                his.append(jnp.where(hit, a_hi, 0.0).astype(BF16))
                los.append(jnp.where(hit, a_lo, 0.0).astype(BF16))
            w = jnp.concatenate(his + los, axis=0)
            g = lax.dot_general(w, hot, (((1,), (1,)), ((), ())),
                                preferred_element_type=F32).astype(BF16)
            g = jnp.concatenate([g[:BLK], g[BLK:]], axis=1)
            tb[pl.ds(pl.multiple_of(f * BLK, 8), BLK), :] = fold(dot(g, hr[...]))
            return c

        lax.fori_loop(0, NF, spread, 0)
        for z in range(ZL):
            phi[which, z] = left_mul(lx[...], tb[pl.ds(z, L, stride=ZP), :])

    orbital(0)
    orbital(1)

    def forward(p):
        other = 1 - p
        for z in range(ZL):
            tb[pl.ds(z, L, stride=ZP), :] = left_mul(lx[...], phi[0, z] * phi[other, z])

        def block(f):
            return right_mul(tb[pl.ds(pl.multiple_of(f * BLK, 8), BLK), :], hr[...])

        def go(d, c):
            f = lax.rem(fft + d, NF)
            send_f[p, f] = block(f)
            copy(send_f.at[p, f], recv_f.at[p, fft], sf.at[p, f], rf.at[p, fft],
                 band, f).start()
            return c

        lax.fori_loop(1, NF, go, 0)
        recv_f[p, fft] = block(fft)

    def solve(p):
        def got(d, c):
            f = lax.rem(fft + d, NF)
            copy(send_f.at[p, f], recv_f.at[p, f], sf.at[p, f], rf.at[p, f],
                 band, f).wait_recv()
            return c

        lax.fori_loop(1, NF, got, 0)
        for x in range(ZL):
            data = recv_f[p, :, x * ZP:(x + 1) * ZP, :].reshape(L, L)
            spec = left_mul(lz1[...], data) * coul[x]
            back = left_mul(lz2[...], spec)
            send_b[p, :, x * ZP:(x + 1) * ZP, :] = back.reshape(NF, ZP, L)

        def go(d, c):
            f = lax.rem(fft + d, NF)
            copy(send_b.at[p, f], recv_b.at[p, fft], sb.at[p, f], rb.at[p, fft],
                 band, f).start()
            return c

        lax.fori_loop(1, NF, go, 0)
        recv_b[p, fft] = send_b[p, fft]

    def backward(p):
        def got(d, c):
            f = lax.rem(fft + d, NF)
            @pl.when(d > 0)
            def _():
                copy(send_b.at[p, f], recv_b.at[p, f], sb.at[p, f], rb.at[p, f],
                     band, f).wait_recv()
            tb2[pl.ds(pl.multiple_of(f * BLK, 8), BLK), :] = right_mul(recv_b[p, f], hr[...])
            return c

        lax.fori_loop(0, NF, got, 0)

    forward(0)
    forward(1)
    solve(0)
    solve(1)
    backward(0)
    for z in range(ZL):
        v = left_mul(lx[...], tb2[pl.ds(z, L, stride=ZP), :])
        acc[z] = (v * phi[1, z])[:N]
        send_v[z] = (v * phi[0, z])[:N]
    to_next = copy(send_v, recv_v, sv, rv, nxt, fft)
    to_next.start()
    backward(1)
    to_next.wait_recv()
    for z in range(ZL):
        v = left_mul(lx[...], tb2[pl.ds(z, L, stride=ZP), :])
        res = (v * phi[0, z])[:N] + acc[z] + recv_v[z]
        tb[pl.ds(z, N, stride=ZP), :] = res

    lane = lax.broadcasted_iota(jnp.int32, (ZP, L), 1)
    total = N * N
    for t in range(-(-total // L)):
        x, off = divmod(t * L, N)
        val = tb[x * ZP:(x + 1) * ZP, :]
        if off:
            val = pltpu.roll(val, L - off, 1)
        if x + 1 < N:
            more = pltpu.roll(tb[(x + 1) * ZP:(x + 2) * ZP, :], N - off, 1)
            val = jnp.where(lane < N - off, val, more)
        width = min(L, total - t * L)
        out[:, t * L:t * L + width] = val[:ZL, :width]

    def left1(d, c):
        b = lax.rem(band + d, NBAND)
        copy(send1.at[b], recv1.at[b], s1.at[b], r1.at[b], b, fft).wait_send()
        return c

    lax.fori_loop(1, NBAND, left1, 0)

    def left2(d, c):
        f = lax.rem(fft + d, NF)
        copy(at_send.at[f], at_recv.at[0, f], s2.at[0, f], r2.at[0, f], band, f).wait_send()
        for p in range(2):
            copy(send_f.at[p, f], recv_f.at[p, f], sf.at[p, f], rf.at[p, f],
                 band, f).wait_send()
            copy(send_b.at[p, f], recv_b.at[p, f], sb.at[p, f], rb.at[p, f],
                 band, f).wait_send()
        return c

    lax.fori_loop(1, NF, left2, 0)

    def left2n(f, c):
        copy(at_send.at[f], at_recv.at[1, f], s2.at[1, f], r2.at[1, f], prv, f).wait_send()
        return c

    lax.fori_loop(0, NF, left2n, 0)
    to_next.wait_send()


def local(coefficients, owned_sticks, stick_counts, stick_columns, band_order):
    tables = [jnp.asarray(t) for t in cas_parts()]
    vmem = pl.BlockSpec(memory_space=pltpu.VMEM)
    dma = pltpu.SemaphoreType.DMA
    out = pl.pallas_call(
        kernel,
        out_shape=jax.ShapeDtypeStruct((ZL, N * N), F32),
        in_specs=[vmem] * 4 + [pl.BlockSpec(memory_space=pltpu.SMEM)] + [vmem] * 5,
        out_specs=vmem,
        scratch_shapes=[
            pltpu.VMEM((NBAND * CAPP, L), F32),
            pltpu.VMEM((NBAND, CAPP, L), F32),
            pltpu.VMEM((NBAND, CAPP, L), F32),
            pltpu.VMEM((NBAND, CAPP, L), F32),
            pltpu.VMEM((STICKS, NBAND * CAPP), BF16),
            pltpu.VMEM((STICKS, L), F32),
            pltpu.VMEM((1, NBAND * CAPP), jnp.int32),
            pltpu.VMEM((8, STP), F32),
            pltpu.VMEM((NF, ZP, STP), F32),
            pltpu.VMEM((2, NF, ZP, STP), F32),
            pltpu.VMEM((2, ZL, L, L), F32),
            pltpu.VMEM((L * ZP, L), F32),
            pltpu.VMEM((L * ZP, L), F32),
            pltpu.VMEM((ZL, L, L), F32),
            pltpu.VMEM((2, NF, BLK, L), F32),
            pltpu.VMEM((2, NF, BLK, L), F32),
            pltpu.VMEM((2, NF, BLK, L), F32),
            pltpu.VMEM((2, NF, BLK, L), F32),
            pltpu.VMEM((ZL, N, L), F32),
            pltpu.VMEM((ZL, N, L), F32),
            pltpu.VMEM((ZL, N, L), F32),
            dma((NBAND,)), dma((NBAND,)),
            dma((2, NF)), dma((2, NF)),
            dma((2, NF)), dma((2, NF)),
            dma((2, NF)), dma((2, NF)),
            dma, dma,
        ],
        compiler_params=pltpu.CompilerParams(
            collective_id=0, has_side_effects=True, vmem_limit_bytes=48 * 1024 * 1024),
    )(coefficients, owned_sticks, stick_counts, stick_columns, band_order, *tables)
    return out[None]


def solution(mesh):
    placed = (P(None, ("band", "fft")), P("fft", None), P("fft", None), P("fft", None), P())
    return jax.shard_map(
        local, mesh=mesh, in_specs=placed, out_specs=P("band", "fft", None), check_vma=False
    )
```

```python
import math

import jax
import jax.numpy as jnp
import ml_dtypes
import numpy as np
from jax import lax
from jax.experimental import pallas as pl
from jax.experimental.pallas import tpu as pltpu
from jax.sharding import PartitionSpec as P

N = 120
NF = 8
NBAND = 32
ZL = N // NF
ZP = 16
CAP = 22
CAPP = 24
STICKS = 352
STP = 384
L = 128
BLK = ZL * ZP
CHUNK = 5
ROUTES = ((0, 4, 6), (4, 4, 1), (8, 4, 7), (12, 3, 0))
EARLY = 5
COULOMB = 0.25
EXCHANGE_FRACTION = 0.25
F32 = jnp.float32
BF16 = jnp.bfloat16


def cas_parts():
    k = np.arange(N)
    angle = (k[:, None] * k[None, :] % N) * (2.0 * math.pi / N)
    full = np.cos(angle) + np.sin(angle)
    zpad = (k // ZL) * ZP + k % ZL

    def parts(a):
        hi = a.astype(ml_dtypes.bfloat16)
        lo = (a - hi.astype(np.float64)).astype(ml_dtypes.bfloat16)
        return hi, lo

    def place(rows, cols):
        out = np.zeros((L, L))
        out[np.ix_(rows, cols)] = full
        return out

    def right(a):
        hi, lo = parts(a)
        row = np.concatenate([hi, lo], axis=1)
        return np.concatenate([row, row], axis=0)

    def left(a):
        hi, lo = parts(a)
        return np.concatenate([hi, lo], axis=1)

    plain = place(k, k)
    return np.concatenate([
        right(plain),
        right(place(k, zpad)),
        left(plain),
        left(place(zpad, k)),
    ], axis=0)


def halves(x):
    hi = x.astype(BF16)
    lo = (x - hi.astype(F32)).astype(BF16)
    return jnp.concatenate([hi, lo], axis=1)


def fold(r):
    return r[:, :L] + r[:, L:]


def dot(a, b):
    return jnp.dot(a, b, preferred_element_type=F32)


def right_mul(x, table):
    return fold(dot(halves(x), table))


def left_mul(table, x):
    cat = halves(x)
    return fold(dot(table, jnp.concatenate([cat, cat], axis=0)))


def kernel(
    coef_h, owned_h, counts_h, cols_h, order_h, tables_h, out,
    coef, owned, counts, cols, order, tables,
    stage, stage3, send1, recv1, sel, keep, owned_p, cols_p, at_send, at_recv, phi, tb, tb2,
    coul, send_f, recv_f3, send_b, recv_b, send_v, recv_v, acc, relay,
    s1, r1, s2, r2, sf, rf, sb, rb, sv, rv, rr, sr, sin,
):
    hr = tables.at[0:2 * L]
    hrz = tables.at[2 * L:4 * L]
    lx = tables.at[4 * L:5 * L]
    lp = tables.at[5 * L:6 * L]
    band = lax.axis_index("band")
    fft = lax.axis_index("fft")
    nxt = lax.rem(band + 1, NBAND)
    prv = lax.rem(band + NBAND - 1, NBAND)

    def copy(src, dst, ssem, rsem, b, f):
        return pltpu.make_async_remote_copy(
            src_ref=src, dst_ref=dst, send_sem=ssem, recv_sem=rsem,
            device_id=(b, f), device_id_type=pl.DeviceIdType.MESH,
        )

    recv_f = recv_f3.reshape(2, L * ZP, L)

    barrier = pltpu.get_barrier_semaphore()

    def hello_band(d, c):
        pl.semaphore_signal(
            barrier, inc=1, device_id=(lax.rem(band + d, NBAND), fft),
            device_id_type=pl.DeviceIdType.MESH)
        return c

    lax.fori_loop(1, NBAND, hello_band, 0)

    def hello_fft(d, c):
        f = lax.rem(fft + d, NF)
        pl.semaphore_signal(
            barrier, inc=1, device_id=(band, f), device_id_type=pl.DeviceIdType.MESH)
        return c

    lax.fori_loop(1, NF, hello_fft, 0)

    loads = [
        pltpu.make_async_copy(src, dst, sin.at[n])
        for n, (src, dst) in enumerate([
            (coef_h, coef), (order_h, order), (owned_h, owned), (counts_h, counts),
            (cols_h, cols), (tables_h, tables)])
    ]
    for load in loads:
        load.start()

    stage[...] = jnp.zeros(stage.shape, F32)
    loads[0].wait()
    for q in range(CAP):
        stage[pl.ds(q, NBAND, stride=CAPP), pl.ds(0, N)] = coef[:, N * q:N * q + N]

    stage3[...] = stage[...].reshape(NBAND, CAPP, L)

    loads[1].wait()

    def reorder(j, c):
        send1[j] = stage3[order[j]]
        return c

    lax.fori_loop(0, NBAND, reorder, 0)

    pl.semaphore_wait(barrier, NBAND - 1 + NF - 1)

    def go1(d, c):
        b = lax.rem(band + d, NBAND)
        copy(send1.at[b], recv1.at[band], s1.at[b], r1.at[band], b, fft).start()
        return c

    lax.fori_loop(1, NBAND, go1, 0)
    recv1[band] = send1[band]

    tb[...] = jnp.zeros(tb.shape, F32)
    tb2[N * ZP:, :] = jnp.zeros(((L - N) * ZP, L), F32)
    for p in range(2):
        recv_f[p, N * ZP:, :] = jnp.zeros(((L - N) * ZP, L), F32)
    for load in loads[2:]:
        load.wait()
    owned_p[...] = jnp.full(owned_p.shape, -1, jnp.int32)
    for o in range(NBAND):
        owned_p[:, CAPP * o:CAPP * o + CAP] = owned[:, CAP * o:CAP * o + CAP]
    rows = lax.broadcasted_iota(jnp.int32, (STICKS, NBAND * CAPP), 0)
    sel[...] = jnp.where(rows == owned_p[...], 1.0, 0.0).astype(BF16)
    cols_p[...] = jnp.full(cols_p.shape, -1.0, F32)
    cols_p[0:1, 0:STICKS] = cols[...].astype(F32)
    cols_p[1:2, 0:STICKS] = counts[...].astype(F32)
    count_b = jnp.transpose(jnp.broadcast_to(cols_p[1:2, :], (L, STP)))[:STICKS]
    kz = lax.broadcasted_iota(jnp.int32, (STICKS, L), 1)
    need = (2 * jnp.minimum(kz, N - kz) + 1).astype(F32)
    keep[...] = jnp.where((kz < N) & (need <= count_b), 1.0, 0.0)
    scale = -EXCHANGE_FRACTION * COULOMB * math.sqrt(N ** 3) / N ** 3
    r0 = lax.broadcasted_iota(jnp.int32, (L, L), 0)
    r1_ = lax.broadcasted_iota(jnp.int32, (L, L), 1)
    mz = jnp.minimum(r0, N - r0)
    my = jnp.minimum(r1_, N - r1_)
    plane = mz * mz + my * my

    def coulomb(x, c):
        kx = fft * ZL + x
        mx = jnp.minimum(kx, N - kx)
        q = (plane + mx * mx).astype(F32)
        coul[x] = jnp.where(q > 0.0, scale / jnp.maximum(q, 1.0), 0.0)
        return c

    lax.fori_loop(0, ZL, coulomb, 0)

    def got1(d, c):
        b = lax.rem(band + d, NBAND)
        copy(send1.at[b], recv1.at[b], s1.at[b], r1.at[b], b, fft).wait_recv()
        return c

    lax.fori_loop(1, NBAND, got1, 0)

    arrived = halves(recv1[...].reshape(NBAND * CAPP, L))
    picked = dot(sel[...], arrived)
    kept = keep[...] > 0.0
    hi = jnp.where(kept, picked[:, :L], 0.0).astype(BF16)
    lo = jnp.where(kept, picked[:, L:], 0.0).astype(BF16)
    along = fold(dot(jnp.concatenate([hi, lo], axis=1), hrz[...]))
    along = jnp.concatenate([along, jnp.zeros((STP - STICKS, L), F32)], axis=0)
    flipped = jnp.transpose(along)
    for f in range(NF):
        at_send[f] = flipped[f * ZP:(f + 1) * ZP]
        at_send[f, ZP - 1:ZP, :] = cols_p[0:1, :]

    def go2(d, c):
        f = lax.rem(fft + d, NF)
        copy(at_send.at[f], at_recv.at[0, fft], s2.at[0, f], r2.at[0, fft], band, f).start()
        return c

    lax.fori_loop(1, NF, go2, 0)
    at_recv[0, fft] = at_send[fft]

    srow = lax.broadcasted_iota(jnp.int32, (ZP, STP), 0)
    kyrow = lax.broadcasted_iota(jnp.int32, (L, STP), 0).astype(F32)

    def arrive(which, d, f):
        if which == 0:
            @pl.when(d > 0)
            def _():
                copy(at_send.at[f], at_recv.at[0, f], s2.at[0, f], r2.at[0, f],
                     band, f).wait_recv()
            copy(at_recv.at[0, f], at_recv.at[1, f], s2.at[1, f], r2.at[1, f],
                 prv, fft).start()
        else:
            copy(at_recv.at[0, f], at_recv.at[1, f], s2.at[1, f], r2.at[1, f],
                 prv, fft).wait_recv()

    def orbital(which):
        def spread(d, c):
            f = lax.rem(fft + d, NF)
            arrive(which, d, f)
            blk = at_recv[which, f]
            col = blk[ZP - 1:ZP, :]
            kx = jnp.floor((col + 0.5) * (1.0 / N))
            ky = col - N * kx
            a = jnp.where(srow < ZL, blk, 0.0)
            hot = jnp.where(kyrow == ky, 1.0, 0.0).astype(BF16)
            a_hi = a.astype(BF16).astype(F32)
            a_lo = a - a_hi
            his, los = [], []
            for x in range(ZL):
                hit = kx == x
                his.append(jnp.where(hit, a_hi, 0.0).astype(BF16))
                los.append(jnp.where(hit, a_lo, 0.0).astype(BF16))
            w = jnp.concatenate(his + los, axis=0)
            g = lax.dot_general(w, hot, (((1,), (1,)), ((), ())),
                                preferred_element_type=F32).astype(BF16)
            g = jnp.concatenate([g[:BLK], g[BLK:]], axis=1)
            tb[pl.ds(pl.multiple_of(f * BLK, 8), BLK), :] = fold(dot(g, hr[...]))
            return c

        lax.fori_loop(0, NF, spread, 0)
        p = 1 - which
        for z in range(ZL):
            value = left_mul(lx[...], tb[pl.ds(z, L, stride=ZP), :])
            phi[which, z] = value
            rho = left_mul(lp[...], value * (value if p else phi[0, z]))
            rho = right_mul(rho, hr[...])
            send_f[p, :, z] = rho.reshape(NF, ZP, L)
            if z % CHUNK == CHUNK - 1:
                first = z - CHUNK + 1

                def go(d, c):
                    f = lax.rem(fft + d, NF)
                    copy(send_f.at[p, f, first:first + CHUNK],
                         recv_f3.at[p, pl.ds(fft * ZL + first, CHUNK)],
                         sf.at[p, f], rf.at[p, fft], band, f).start()
                    return c

                lax.fori_loop(1, NF, go, 0)
        recv_f3[p, pl.ds(fft * ZL, ZL)] = send_f[p, fft]

    def solve(p, upto):
        def got(d, c):
            f = lax.rem(fft + d, NF)
            copy(send_f.at[p, f], recv_f3.at[p, pl.ds(f * ZL, ZL)],
                 sf.at[p, f], rf.at[p, f], band, f).wait_recv()
            return c

        lax.fori_loop(1, NF, got, 0)
        for x in range(ZL):
            data = recv_f[p, pl.ds(x, L, stride=ZP), :]
            spec = left_mul(lx[...], data) * coul[x]
            send_b[p, :, x] = left_mul(lp[...], spec).reshape(NF, ZP, L)
            if x % CHUNK == CHUNK - 1 and x < upto:
                give(p, x - CHUNK + 1)

    def give(p, first):
        def go(d, c):
            f = lax.rem(fft + d, NF)
            copy(send_b.at[p, f, first:first + CHUNK],
                 recv_b.at[p, fft, first:first + CHUNK],
                 sb.at[p, f], rb.at[p, fft], band, f).start()
            return c

        lax.fori_loop(1, NF, go, 0)

    def backward(p):
        def got(d, c):
            f = lax.rem(fft + d, NF)
            copy(send_b.at[p, f], recv_b.at[p, f], sb.at[p, f], rb.at[p, f],
                 band, f).wait_recv()
            tb2[pl.ds(pl.multiple_of(f * BLK, 8), BLK), :] = right_mul(
                recv_b[p, f].reshape(BLK, L), hr[...])
            return c

        tb2[pl.ds(pl.multiple_of(fft * BLK, 8), BLK), :] = right_mul(
            send_b[p, fft].reshape(BLK, L), hr[...])
        lax.fori_loop(1, NF, got, 0)

    orbital(0)
    orbital(1)
    solve(1, EARLY)
    solve(0, ZL)
    for first in range(EARLY, ZL, CHUNK):
        give(1, first)
    backward(0)
    far = lax.rem(band, 16) == 15
    nxt_row = (nxt // 16) * 16

    def to_next(first, count):
        return copy(send_v.at[pl.ds(first, count)], recv_v.at[pl.ds(first, count)],
                    sv, rv, nxt, fft)

    def to_relay(first, count, hop):
        return copy(send_v.at[pl.ds(first, count)], relay.at[pl.ds(0, count)],
                    sv, rr, nxt_row + 2 * hop, fft)

    def from_relay(first, count):
        return copy(relay.at[pl.ds(0, count)], recv_v.at[pl.ds(first, count)],
                    sr, rv, (band // 16) * 16, fft)

    def send_term(first, count, hop):
        if hop == 0:
            to_next(first, count).start()
        else:
            @pl.when(far)
            def _():
                to_relay(first, count, hop).start()

            @pl.when(jnp.logical_not(far))
            def _():
                to_next(first, count).start()

    for first, count, hop in ROUTES:
        for z in range(first, first + count):
            v = left_mul(lx[...], tb2[pl.ds(z, L, stride=ZP), :])
            acc[z] = (v * phi[1, z])[:N]
            send_v[z] = (v * phi[0, z])[:N]
        send_term(first, count, hop)
    for first, count, hop in ROUTES:
        if hop:
            @pl.when(lax.rem(band, 16) == 2 * hop)
            def _():
                to_relay(first, count, hop).wait_recv()
                from_relay(first, count).start()

    backward(1)
    for z in range(ZL):
        v = left_mul(lx[...], tb2[pl.ds(z, L, stride=ZP), :])
        acc[z] += (v * phi[0, z])[:N]
    to_next(0, ZL).wait_recv()
    for z in range(ZL):
        tb[pl.ds(z, N, stride=ZP), :] = acc[z] + recv_v[z]

    lane = lax.broadcasted_iota(jnp.int32, (ZP, L), 1)
    total = N * N
    for t in range(-(-total // L)):
        x, off = divmod(t * L, N)
        val = tb[x * ZP:(x + 1) * ZP, :]
        if off:
            val = pltpu.roll(val, L - off, 1)
        if x + 1 < N:
            more = pltpu.roll(tb[(x + 1) * ZP:(x + 2) * ZP, :], N - off, 1)
            val = jnp.where(lane < N - off, val, more)
        width = min(L, total - t * L)
        out[:, 0, t * L:t * L + width] = val[:ZL, :width]

    def left1(d, c):
        b = lax.rem(band + d, NBAND)
        copy(send1.at[b], recv1.at[b], s1.at[b], r1.at[b], b, fft).wait_send()
        return c

    lax.fori_loop(1, NBAND, left1, 0)

    def left2(d, c):
        f = lax.rem(fft + d, NF)
        copy(at_send.at[f], at_recv.at[0, f], s2.at[0, f], r2.at[0, f], band, f).wait_send()
        for p in range(2):
            copy(send_f.at[p, f], recv_f3.at[p, pl.ds(f * ZL, ZL)], sf.at[p, f], rf.at[p, f],
                 band, f).wait_send()
            copy(send_b.at[p, f], recv_b.at[p, f], sb.at[p, f], rb.at[p, f],
                 band, f).wait_send()
        return c

    lax.fori_loop(1, NF, left2, 0)

    def left2n(f, c):
        copy(at_recv.at[0, f], at_recv.at[1, f], s2.at[1, f], r2.at[1, f],
             prv, fft).wait_send()
        return c

    lax.fori_loop(0, NF, left2n, 0)
    to_next(0, ZL).wait_send()
    for first, count, hop in ROUTES:
        if hop:
            @pl.when(lax.rem(band, 16) == 2 * hop)
            def _():
                from_relay(first, count).wait_send()


def local(coefficients, owned_sticks, stick_counts, stick_columns, band_order):
    tables = jnp.asarray(cas_parts())
    vmem = pl.BlockSpec(memory_space=pltpu.VMEM)
    dma = pltpu.SemaphoreType.DMA
    out = pl.pallas_call(
        kernel,
        out_shape=jax.ShapeDtypeStruct((ZL, 1, N * N), F32),
        in_specs=[pl.BlockSpec(memory_space=pltpu.HBM)] * 6,
        out_specs=vmem,
        scratch_shapes=[
            pltpu.VMEM((NBAND, CAP * N), F32),
            pltpu.VMEM((1, NBAND * CAP), jnp.int32),
            pltpu.VMEM((1, STICKS), jnp.int32),
            pltpu.VMEM((1, STICKS), jnp.int32),
            pltpu.SMEM((NBAND,), jnp.int32),
            pltpu.VMEM((6 * L, 2 * L), BF16),
            pltpu.VMEM((NBAND * CAPP, L), F32),
            pltpu.VMEM((NBAND, CAPP, L), F32),
            pltpu.VMEM((NBAND, CAPP, L), F32),
            pltpu.VMEM((NBAND, CAPP, L), F32),
            pltpu.VMEM((STICKS, NBAND * CAPP), BF16),
            pltpu.VMEM((STICKS, L), F32),
            pltpu.VMEM((1, NBAND * CAPP), jnp.int32),
            pltpu.VMEM((8, STP), F32),
            pltpu.VMEM((NF, ZP, STP), F32),
            pltpu.VMEM((2, NF, ZP, STP), F32),
            pltpu.VMEM((2, ZL, L, L), F32),
            pltpu.VMEM((L * ZP, L), F32),
            pltpu.VMEM((L * ZP, L), F32),
            pltpu.VMEM((ZL, L, L), F32),
            pltpu.VMEM((2, NF, ZL, ZP, L), F32),
            pltpu.VMEM((2, L, ZP, L), F32),
            pltpu.VMEM((2, NF, ZL, ZP, L), F32),
            pltpu.VMEM((2, NF, ZL, ZP, L), F32),
            pltpu.VMEM((ZL, N, L), F32),
            pltpu.VMEM((ZL, N, L), F32),
            pltpu.VMEM((ZL, N, L), F32),
            pltpu.VMEM((4, N, L), F32),
            dma((NBAND,)), dma((NBAND,)),
            dma((2, NF)), dma((2, NF)),
            dma((2, NF)), dma((2, NF)),
            dma((2, NF)), dma((2, NF)),
            dma, dma, dma, dma,
            dma((6,)),
        ],
        compiler_params=pltpu.CompilerParams(
            collective_id=0, has_side_effects=True, vmem_limit_bytes=60 * 1024 * 1024),
    )(coefficients, owned_sticks, stick_counts, stick_columns, band_order, tables)
    return out.reshape(1, ZL, N * N)


def solution(mesh):
    placed = (P(None, ("band", "fft")), P("fft", None), P("fft", None), P("fft", None), P())
    return jax.shard_map(
        local, mesh=mesh, in_specs=placed, out_specs=P("band", "fft", None), check_vma=False
    )
```

```python
import math

import jax
import jax.numpy as jnp
import ml_dtypes
import numpy as np
from jax import lax
from jax.experimental import pallas as pl
from jax.experimental.pallas import tpu as pltpu
from jax.sharding import PartitionSpec as P

N = 120
NF = 8
NBAND = 32
ZL = N // NF
ZP = 16
CAP = 22
CAPP = 24
STICKS = 352
STP = 384
L = 128
BLK = ZL * ZP
CHUNK = 5
PARTS = ZL // CHUNK
ROUTES = ((0, 4, 6), (4, 4, 1), (8, 4, 7), (12, 3, 0))
COULOMB = 0.25
EXCHANGE_FRACTION = 0.25
F32 = jnp.float32
BF16 = jnp.bfloat16


def cas_parts():
    k = np.arange(N)
    angle = (k[:, None] * k[None, :] % N) * (2.0 * math.pi / N)
    full = np.cos(angle) + np.sin(angle)
    zpad = (k // ZL) * ZP + k % ZL

    def parts(a):
        hi = a.astype(ml_dtypes.bfloat16)
        lo = (a - hi.astype(np.float64)).astype(ml_dtypes.bfloat16)
        return hi, lo

    def place(rows, cols):
        out = np.zeros((L, L))
        out[np.ix_(rows, cols)] = full
        return out

    def right(a):
        hi, lo = parts(a)
        row = np.concatenate([hi, lo], axis=1)
        return np.concatenate([row, row], axis=0)

    def left(a):
        hi, lo = parts(a)
        return np.concatenate([hi, lo], axis=1)

    plain = place(k, k)
    return np.concatenate([
        right(plain),
        right(place(k, zpad)),
        left(plain),
        left(place(zpad, k)),
    ], axis=0)


def halves(x):
    hi = x.astype(BF16)
    lo = (x - hi.astype(F32)).astype(BF16)
    return jnp.concatenate([hi, lo], axis=1)


def fold(r):
    return r[:, :L] + r[:, L:]


def dot(a, b):
    return jnp.dot(a, b, preferred_element_type=F32)


def right_mul(x, table):
    return fold(dot(halves(x), table))


def left_mul(table, x):
    cat = halves(x)
    return fold(dot(table, jnp.concatenate([cat, cat], axis=0)))


def kernel(
    coef_h, owned_h, counts_h, cols_h, order_h, tables_h, out,
    coef, owned, counts, cols, order, tables,
    stage, stage3, send1, recv1, sel, keep, owned_p, row_p, all_cols, kx_of, along_y, at_send, at_recv, phi, tb, tb2,
    coul, send_f, recv_f3, send_b, recv_b, send_v, recv_v, acc, relay,
    sk, rk, s1, r1, s2, r2, sp, rf, rb, sv, rv, rr, sr, sin,
):
    hr = tables.at[0:2 * L]
    hrz = tables.at[2 * L:4 * L]
    lx = tables.at[4 * L:5 * L]
    lp = tables.at[5 * L:6 * L]
    band = lax.axis_index("band")
    fft = lax.axis_index("fft")
    nxt = lax.rem(band + 1, NBAND)
    prv = lax.rem(band + NBAND - 1, NBAND)

    def copy(src, dst, ssem, rsem, b, f):
        return pltpu.make_async_remote_copy(
            src_ref=src, dst_ref=dst, send_sem=ssem, recv_sem=rsem,
            device_id=(b, f), device_id_type=pl.DeviceIdType.MESH,
        )

    recv_f = recv_f3.reshape(2, L * ZP, L)

    barrier = pltpu.get_barrier_semaphore()

    def hello_band(d, c):
        pl.semaphore_signal(
            barrier, inc=1, device_id=(lax.rem(band + d, NBAND), fft),
            device_id_type=pl.DeviceIdType.MESH)
        return c

    lax.fori_loop(1, NBAND, hello_band, 0)

    def hello_fft(d, c):
        f = lax.rem(fft + d, NF)
        pl.semaphore_signal(
            barrier, inc=1, device_id=(band, f), device_id_type=pl.DeviceIdType.MESH)
        pl.semaphore_signal(
            barrier, inc=1, device_id=(nxt, f), device_id_type=pl.DeviceIdType.MESH)
        return c

    lax.fori_loop(1, NF, hello_fft, 0)

    loads = [
        pltpu.make_async_copy(src, dst, sin.at[n])
        for n, (src, dst) in enumerate([
            (coef_h, coef), (order_h, order), (owned_h, owned), (counts_h, counts),
            (cols_h, cols), (tables_h, tables)])
    ]
    for load in loads:
        load.start()

    stage[...] = jnp.zeros(stage.shape, F32)
    loads[0].wait()
    for q in range(CAP):
        stage[pl.ds(q, NBAND, stride=CAPP), pl.ds(0, N)] = coef[:, N * q:N * q + N]

    stage3[...] = stage[...].reshape(NBAND, CAPP, L)

    loads[1].wait()

    def reorder(j, c):
        send1[j] = stage3[order[j]]
        return c

    lax.fori_loop(0, NBAND, reorder, 0)

    pl.semaphore_wait(barrier, NBAND - 1 + 2 * (NF - 1))

    loads[4].wait()
    all_cols[fft] = cols[...]

    def go0(d, c):
        f = lax.rem(fft + d, NF)
        copy(cols, all_cols.at[fft], sk.at[f], rk.at[fft], band, f).start()
        return c

    lax.fori_loop(1, NF, go0, 0)

    def go1(d, c):
        b = lax.rem(band + d, NBAND)
        copy(send1.at[b], recv1.at[band], s1.at[b], r1.at[band], b, fft).start()
        return c

    lax.fori_loop(1, NBAND, go1, 0)
    recv1[band] = send1[band]

    tb[...] = jnp.zeros(tb.shape, F32)
    tb2[N * ZP:, :] = jnp.zeros(((L - N) * ZP, L), F32)
    for p in range(2):
        recv_f[p, N * ZP:, :] = jnp.zeros(((L - N) * ZP, L), F32)
    for n in (2, 3, 5):
        loads[n].wait()
    owned_p[...] = jnp.full(owned_p.shape, -1, jnp.int32)
    for o in range(NBAND):
        owned_p[:, CAPP * o:CAPP * o + CAP] = owned[:, CAP * o:CAP * o + CAP]
    rows = lax.broadcasted_iota(jnp.int32, (STICKS, NBAND * CAPP), 0)
    sel[...] = jnp.where(rows == owned_p[...], 1.0, 0.0).astype(BF16)
    row_p[...] = jnp.full(row_p.shape, -1.0, F32)
    row_p[0:1, 0:STICKS] = counts[...].astype(F32)
    count_b = jnp.transpose(jnp.broadcast_to(row_p[0:1, :], (L, STP)))[:STICKS]
    kz = lax.broadcasted_iota(jnp.int32, (STICKS, L), 1)
    need = (2 * jnp.minimum(kz, N - kz) + 1).astype(F32)
    keep[...] = jnp.where((kz < N) & (need <= count_b), 1.0, 0.0)
    scale = -EXCHANGE_FRACTION * COULOMB * math.sqrt(N ** 3) / N ** 3
    r0 = lax.broadcasted_iota(jnp.int32, (L, L), 0)
    r1_ = lax.broadcasted_iota(jnp.int32, (L, L), 1)
    mz = jnp.minimum(r0, N - r0)
    my = jnp.minimum(r1_, N - r1_)
    plane = mz * mz + my * my

    def coulomb(x, c):
        kx = fft * ZL + x
        mx = jnp.minimum(kx, N - kx)
        q = (plane + mx * mx).astype(F32)
        coul[x] = jnp.where(q > 0.0, scale / jnp.maximum(q, 1.0), 0.0)
        return c

    lax.fori_loop(0, ZL, coulomb, 0)

    def got0(d, c):
        f = lax.rem(fft + d, NF)
        copy(cols, all_cols.at[f], sk.at[f], rk.at[f], band, f).wait_recv()
        return c

    lax.fori_loop(1, NF, got0, 0)
    lane_s = lax.broadcasted_iota(jnp.int32, (STP, L), 1).astype(F32)

    def ready(f, c):
        row_p[1:2, 0:STICKS] = all_cols[f].astype(F32)
        col = row_p[1:2, :]
        kx = jnp.floor((col + 0.5) * (1.0 / N))
        kx_of[f] = kx
        ky = jnp.transpose(jnp.broadcast_to(col - N * kx, (L, STP)))
        hot = jnp.where(lane_s == ky, 1.0, 0.0).astype(BF16)
        along_y[f] = dot(hot, hr[0:L]).astype(BF16)
        return c

    lax.fori_loop(0, NF, ready, 0)

    def got1(d, c):
        b = lax.rem(band + d, NBAND)
        copy(send1.at[b], recv1.at[b], s1.at[b], r1.at[b], b, fft).wait_recv()
        return c

    lax.fori_loop(1, NBAND, got1, 0)

    arrived = halves(recv1[...].reshape(NBAND * CAPP, L))
    picked = dot(sel[...], arrived)
    kept = keep[...] > 0.0
    hi = jnp.where(kept, picked[:, :L], 0.0).astype(BF16)
    lo = jnp.where(kept, picked[:, L:], 0.0).astype(BF16)
    along = fold(dot(jnp.concatenate([hi, lo], axis=1), hrz[...]))
    along = jnp.concatenate([along, jnp.zeros((STP - STICKS, L), F32)], axis=0)
    flipped = jnp.transpose(along)
    for f in range(NF):
        at_send[f] = flipped[f * ZP:(f + 1) * ZP]

    def go2(d, c):
        f = lax.rem(fft + d, NF)
        copy(at_send.at[f], at_recv.at[0, fft], s2.at[0, f], r2.at[0, fft], band, f).start()
        return c

    lax.fori_loop(1, NF, go2, 0)
    at_recv[0, fft] = at_send[fft]

    def go2n(d, c):
        f = lax.rem(fft + d, NF)
        copy(at_send.at[f], at_recv.at[1, fft], s2.at[1, f], r2.at[1, fft], prv, f).start()
        return c

    lax.fori_loop(0, NF, go2n, 0)

    def spread(which, f):
        kx = kx_of[f]
        a = at_recv[which, f]
        a_hi = a.astype(BF16).astype(F32)
        a_lo = a - a_hi
        w = [jnp.where(kx == x, part, 0.0).astype(BF16)
             for part in (a_hi, a_lo) for x in range(ZL)]
        g = fold(dot(jnp.concatenate(w, axis=0), along_y[f]))
        tb[f * BLK:(f + 1) * BLK, :] = g[:BLK] + g[BLK:]

    def stick_block(which, d, b, f):
        return copy(at_send.at[f], at_recv.at[which, f], s2.at[which, f], r2.at[which, f], b, f)

    def own_arrives(d, c):
        f = lax.rem(fft + d, NF)
        stick_block(0, d, band, f).wait_recv()
        return c

    def next_arrives(f, c):
        stick_block(1, f, nxt, f).wait_recv()
        return c

    def part(k, f):
        step, first = k // PARTS, k % PARTS * CHUNK
        p = step % 2
        if step < 2:
            return copy(send_f.at[p, f, first:first + CHUNK],
                        recv_f3.at[p, pl.ds(fft * ZL + first, CHUNK)],
                        sp.at[k, f], rf.at[p, fft], band, f)
        return copy(send_b.at[p, f, first:first + CHUNK],
                    recv_b.at[p, fft, first:first + CHUNK],
                    sp.at[k, f], rb.at[p, fft], band, f)

    def each_other(act):
        lax.fori_loop(1, NF, lambda d, c: (act(lax.rem(fft + d, NF)), c)[1], 0)

    def issue(k):
        if k >= 2:
            each_other(lambda f: part(k - 2, f).wait_send())
        each_other(lambda f: part(k, f).start())

    def forward(p, first, count):
        for z in range(first, first + count):
            rho = left_mul(lp[...], phi[0, z] * phi[1 - p, z])
            send_f[p, :, z] = right_mul(rho, hr[...]).reshape(NF, ZP, L)

    def orbital(which, first, count):
        for z in range(first, first + count):
            phi[which, z] = left_mul(lx[...], tb[pl.ds(z, L, stride=ZP), :])

    def solve(p):
        recv_f3[p, pl.ds(fft * ZL, ZL)] = send_f[p, fft]
        each_other(lambda f: copy(
            send_f.at[p, f], recv_f3.at[p, pl.ds(f * ZL, ZL)],
            sp.at[0, f], rf.at[p, f], band, f).wait_recv())
        for x in range(ZL):
            data = recv_f[p, pl.ds(x, L, stride=ZP), :]
            spec = left_mul(lx[...], data) * coul[x]
            send_b[p, :, x] = left_mul(lp[...], spec).reshape(NF, ZP, L)

    def backward(p):
        def got(d, c):
            f = lax.rem(fft + d, NF)
            copy(send_b.at[p, f], recv_b.at[p, f], sp.at[0, f], rb.at[p, f],
                 band, f).wait_recv()
            return c

        recv_b[p, fft] = send_b[p, fft]
        lax.fori_loop(1, NF, got, 0)
        for f in range(NF):
            tb2[f * BLK:(f + 1) * BLK, :] = right_mul(recv_b[p, f].reshape(BLK, L), hr[...])

    lax.fori_loop(1, NF, own_arrives, 0)
    for f in range(NF):
        spread(0, f)
    orbital(0, 0, ZL)
    lax.fori_loop(0, NF, next_arrives, 0)
    for f in range(NF):
        spread(1, f)
    for n in range(PARTS):
        orbital(1, n * CHUNK, CHUNK)
        forward(0, n * CHUNK, CHUNK)
        if n < 2:
            issue(n)
    forward(1, 0, ZL)
    for k in range(2, 5):
        issue(k)
    solve(0)
    for k in range(5, 8):
        issue(k)
    solve(1)
    for k in range(8, 11):
        issue(k)
    backward(0)
    far = lax.rem(band, 16) == 15
    nxt_row = (nxt // 16) * 16

    def to_next(first, count):
        return copy(send_v.at[pl.ds(first, count)], recv_v.at[pl.ds(first, count)],
                    sv, rv, nxt, fft)

    def to_relay(first, count, hop):
        return copy(send_v.at[pl.ds(first, count)], relay.at[pl.ds(0, count)],
                    sv, rr, nxt_row + 2 * hop, fft)

    def from_relay(first, count):
        return copy(relay.at[pl.ds(0, count)], recv_v.at[pl.ds(first, count)],
                    sr, rv, (band // 16) * 16, fft)

    def send_term(first, count, hop):
        if hop == 0:
            to_next(first, count).start()
        else:
            @pl.when(far)
            def _():
                to_relay(first, count, hop).start()

            @pl.when(jnp.logical_not(far))
            def _():
                to_next(first, count).start()

    for first, count, hop in ROUTES:
        for z in range(first, first + count):
            v = left_mul(lx[...], tb2[pl.ds(z, L, stride=ZP), :])
            acc[z] = (v * phi[1, z])[:N]
            send_v[z] = (v * phi[0, z])[:N]
        send_term(first, count, hop)
    issue(11)
    for first, count, hop in ROUTES:
        if hop:
            @pl.when(lax.rem(band, 16) == 2 * hop)
            def _():
                to_relay(first, count, hop).wait_recv()
                from_relay(first, count).start()

    backward(1)
    for z in range(ZL):
        v = left_mul(lx[...], tb2[pl.ds(z, L, stride=ZP), :])
        acc[z] += (v * phi[0, z])[:N]
    to_next(0, ZL).wait_recv()
    for z in range(ZL):
        tb[pl.ds(z, N, stride=ZP), :] = acc[z] + recv_v[z]

    lane = lax.broadcasted_iota(jnp.int32, (ZP, L), 1)
    total = N * N
    for t in range(-(-total // L)):
        x, off = divmod(t * L, N)
        val = tb[x * ZP:(x + 1) * ZP, :]
        if off:
            val = pltpu.roll(val, L - off, 1)
        if x + 1 < N:
            more = pltpu.roll(tb[(x + 1) * ZP:(x + 2) * ZP, :], N - off, 1)
            val = jnp.where(lane < N - off, val, more)
        width = min(L, total - t * L)
        out[:, 0, t * L:t * L + width] = val[:ZL, :width]

    def left1(d, c):
        b = lax.rem(band + d, NBAND)
        copy(send1.at[b], recv1.at[b], s1.at[b], r1.at[b], b, fft).wait_send()
        return c

    lax.fori_loop(1, NBAND, left1, 0)

    def left2(d, c):
        f = lax.rem(fft + d, NF)
        copy(cols, all_cols.at[f], sk.at[f], rk.at[f], band, f).wait_send()
        stick_block(0, d, band, f).wait_send()
        for k in (10, 11):
            part(k, f).wait_send()
        return c

    lax.fori_loop(1, NF, left2, 0)

    def left2n(f, c):
        stick_block(1, f, prv, f).wait_send()
        return c

    lax.fori_loop(0, NF, left2n, 0)
    to_next(0, ZL).wait_send()
    for first, count, hop in ROUTES:
        if hop:
            @pl.when(lax.rem(band, 16) == 2 * hop)
            def _():
                from_relay(first, count).wait_send()


def local(coefficients, owned_sticks, stick_counts, stick_columns, band_order):
    tables = jnp.asarray(cas_parts())
    vmem = pl.BlockSpec(memory_space=pltpu.VMEM)
    dma = pltpu.SemaphoreType.DMA
    out = pl.pallas_call(
        kernel,
        out_shape=jax.ShapeDtypeStruct((ZL, 1, N * N), F32),
        in_specs=[pl.BlockSpec(memory_space=pltpu.HBM)] * 6,
        out_specs=vmem,
        scratch_shapes=[
            pltpu.VMEM((NBAND, CAP * N), F32),
            pltpu.VMEM((1, NBAND * CAP), jnp.int32),
            pltpu.VMEM((1, STICKS), jnp.int32),
            pltpu.VMEM((1, STICKS), jnp.int32),
            pltpu.SMEM((NBAND,), jnp.int32),
            pltpu.VMEM((6 * L, 2 * L), BF16),
            pltpu.VMEM((NBAND * CAPP, L), F32),
            pltpu.VMEM((NBAND, CAPP, L), F32),
            pltpu.VMEM((NBAND, CAPP, L), F32),
            pltpu.VMEM((NBAND, CAPP, L), F32),
            pltpu.VMEM((STICKS, NBAND * CAPP), BF16),
            pltpu.VMEM((STICKS, L), F32),
            pltpu.VMEM((1, NBAND * CAPP), jnp.int32),
            pltpu.VMEM((8, STP), F32),
            pltpu.VMEM((NF, 1, STICKS), jnp.int32),
            pltpu.VMEM((NF, 1, STP), F32),
            pltpu.VMEM((NF, STP, 2 * L), BF16),
            pltpu.VMEM((NF, ZP, STP), F32),
            pltpu.VMEM((2, NF, ZP, STP), F32),
            pltpu.VMEM((2, ZL, L, L), F32),
            pltpu.VMEM((L * ZP, L), F32),
            pltpu.VMEM((L * ZP, L), F32),
            pltpu.VMEM((ZL, L, L), F32),
            pltpu.VMEM((2, NF, ZL, ZP, L), F32),
            pltpu.VMEM((2, L, ZP, L), F32),
            pltpu.VMEM((2, NF, ZL, ZP, L), F32),
            pltpu.VMEM((2, NF, ZL, ZP, L), F32),
            pltpu.VMEM((ZL, N, L), F32),
            pltpu.VMEM((ZL, N, L), F32),
            pltpu.VMEM((ZL, N, L), F32),
            pltpu.VMEM((4, N, L), F32),
            dma((NF,)), dma((NF,)),
            dma((NBAND,)), dma((NBAND,)),
            dma((2, NF)), dma((2, NF)),
            dma((4 * PARTS, NF)), dma((2, NF)), dma((2, NF)),
            dma, dma, dma, dma,
            dma((6,)),
        ],
        compiler_params=pltpu.CompilerParams(
            collective_id=0, has_side_effects=True, vmem_limit_bytes=48 * 1024 * 1024),
    )(*[pltpu.with_memory_space_constraint(a, pltpu.HBM) for a in (
        coefficients, owned_sticks, stick_counts, stick_columns, band_order, tables)])
    return out.reshape(1, ZL, N * N)


def solution(mesh):
    placed = (P(None, ("band", "fft")), P("fft", None), P("fft", None), P("fft", None), P())
    return jax.shard_map(
        local, mesh=mesh, in_specs=placed, out_specs=P("band", "fft", None), check_vma=False
    )
```

```python
import math

import jax
import jax.numpy as jnp
import ml_dtypes
import numpy as np
from jax import lax
from jax.experimental import pallas as pl
from jax.experimental.pallas import tpu as pltpu
from jax.sharding import PartitionSpec as P

N = 120
NF = 8
NBAND = 32
ZL = N // NF
ZP = 16
CAP = 22
CAPP = 24
STICKS = 352
STP = 384
L = 128
BLK = ZL * ZP
CHUNK = 5
PARTS = ZL // CHUNK
ROUTES = ((0, 4, 6), (4, 4, 1), (8, 4, 7), (12, 3, 0))
COULOMB = 0.25
EXCHANGE_FRACTION = 0.25
F32 = jnp.float32
BF16 = jnp.bfloat16


def cas_parts():
    k = np.arange(N)
    angle = (k[:, None] * k[None, :] % N) * (2.0 * math.pi / N)
    full = np.cos(angle) + np.sin(angle)
    zpad = (k // ZL) * ZP + k % ZL

    def parts(a):
        hi = a.astype(ml_dtypes.bfloat16)
        lo = (a - hi.astype(np.float64)).astype(ml_dtypes.bfloat16)
        return hi, lo

    def place(rows, cols):
        out = np.zeros((L, L))
        out[np.ix_(rows, cols)] = full
        return out

    def right(a):
        hi, lo = parts(a)
        row = np.concatenate([hi, lo], axis=1)
        return np.concatenate([row, row], axis=0)

    def left(a):
        hi, lo = parts(a)
        return np.concatenate([hi, lo], axis=1)

    plain = place(k, k)
    return np.concatenate([
        right(plain),
        right(place(k, zpad)),
        left(plain),
        left(place(zpad, k)),
        left(place(k, zpad)),
    ], axis=0)


def halves(x):
    hi = x.astype(BF16)
    lo = (x - hi.astype(F32)).astype(BF16)
    return jnp.concatenate([hi, lo], axis=1)


def fold(r):
    return r[:, :L] + r[:, L:]


def dot(a, b):
    return jnp.dot(a, b, preferred_element_type=F32)


def right_mul(x, table):
    return fold(dot(halves(x), table))


def left_mul(table, x):
    cat = halves(x)
    return fold(dot(table, jnp.concatenate([cat, cat], axis=0)))


def kernel(
    coef_h, owned_h, counts_h, cols_h, order_h, tables_h, out,
    coef, owned, counts, cols, order, tables,
    stage, stage3, send1, recv1, sel, keep, owned_p, row_p, all_cols, kx_of, along_y, at_send, at_recv, phi, tb, tb2,
    coul, send_f, recv_f, send_b, recv_b, send_v, recv_v, acc, relay,
    sk, rk, s1, r1, s2, r2, sp, rf, rb, sv, rv, rr, sr, sin,
):
    hr = tables.at[0:2 * L]
    hrz = tables.at[2 * L:4 * L]
    lx = tables.at[4 * L:5 * L]
    lp = tables.at[5 * L:6 * L]
    lz = tables.at[6 * L:7 * L]
    band = lax.axis_index("band")
    fft = lax.axis_index("fft")
    nxt = lax.rem(band + 1, NBAND)
    prv = lax.rem(band + NBAND - 1, NBAND)

    def copy(src, dst, ssem, rsem, b, f):
        return pltpu.make_async_remote_copy(
            src_ref=src, dst_ref=dst, send_sem=ssem, recv_sem=rsem,
            device_id=(b, f), device_id_type=pl.DeviceIdType.MESH,
        )

    barrier = pltpu.get_barrier_semaphore()

    def hello_band(d, c):
        pl.semaphore_signal(
            barrier, inc=1, device_id=(lax.rem(band + d, NBAND), fft),
            device_id_type=pl.DeviceIdType.MESH)
        return c

    lax.fori_loop(1, NBAND, hello_band, 0)

    def hello_fft(d, c):
        f = lax.rem(fft + d, NF)
        pl.semaphore_signal(
            barrier, inc=1, device_id=(band, f), device_id_type=pl.DeviceIdType.MESH)
        pl.semaphore_signal(
            barrier, inc=1, device_id=(nxt, f), device_id_type=pl.DeviceIdType.MESH)
        return c

    lax.fori_loop(1, NF, hello_fft, 0)

    loads = [
        pltpu.make_async_copy(src, dst, sin.at[n])
        for n, (src, dst) in enumerate([
            (coef_h, coef), (order_h, order), (owned_h, owned), (counts_h, counts),
            (cols_h, cols), (tables_h, tables)])
    ]
    for load in loads:
        load.start()

    stage[...] = jnp.zeros(stage.shape, F32)
    loads[0].wait()
    for q in range(CAP):
        stage[pl.ds(q, NBAND, stride=CAPP), pl.ds(0, N)] = coef[:, N * q:N * q + N]

    stage3[...] = stage[...].reshape(NBAND, CAPP, L)

    loads[1].wait()

    def reorder(j, c):
        send1[j] = stage3[order[j]]
        return c

    lax.fori_loop(0, NBAND, reorder, 0)

    pl.semaphore_wait(barrier, NBAND - 1 + 2 * (NF - 1))

    loads[4].wait()
    all_cols[fft] = cols[...]

    def go0(d, c):
        f = lax.rem(fft + d, NF)
        copy(cols, all_cols.at[fft], sk.at[f], rk.at[fft], band, f).start()
        return c

    lax.fori_loop(1, NF, go0, 0)

    def go1(d, c):
        b = lax.rem(band + d, NBAND)
        copy(send1.at[b], recv1.at[band], s1.at[b], r1.at[band], b, fft).start()
        return c

    lax.fori_loop(1, NBAND, go1, 0)
    recv1[band] = send1[band]

    tb[...] = jnp.zeros(tb.shape, F32)
    tb2[N * ZP:, :] = jnp.zeros(((L - N) * ZP, L), F32)
    for n in (2, 3, 5):
        loads[n].wait()
    owned_p[...] = jnp.full(owned_p.shape, -1, jnp.int32)
    for o in range(NBAND):
        owned_p[:, CAPP * o:CAPP * o + CAP] = owned[:, CAP * o:CAP * o + CAP]
    rows = lax.broadcasted_iota(jnp.int32, (STICKS, NBAND * CAPP), 0)
    sel[...] = jnp.where(rows == owned_p[...], 1.0, 0.0).astype(BF16)
    row_p[...] = jnp.full(row_p.shape, -1.0, F32)
    row_p[0:1, 0:STICKS] = counts[...].astype(F32)
    count_b = jnp.transpose(jnp.broadcast_to(row_p[0:1, :], (L, STP)))[:STICKS]
    kz = lax.broadcasted_iota(jnp.int32, (STICKS, L), 1)
    need = (2 * jnp.minimum(kz, N - kz) + 1).astype(F32)
    keep[...] = jnp.where((kz < N) & (need <= count_b), 1.0, 0.0)
    scale = -EXCHANGE_FRACTION * COULOMB * math.sqrt(N ** 3) / N ** 3
    r0 = lax.broadcasted_iota(jnp.int32, (L, L), 0)
    r1_ = lax.broadcasted_iota(jnp.int32, (L, L), 1)
    mz = jnp.minimum(r0, N - r0)
    my = jnp.minimum(r1_, N - r1_)
    plane = mz * mz + my * my

    def coulomb(x, c):
        kx = fft * ZL + x
        mx = jnp.minimum(kx, N - kx)
        q = (plane + mx * mx).astype(F32)
        coul[x] = jnp.where(q > 0.0, scale / jnp.maximum(q, 1.0), 0.0)
        return c

    lax.fori_loop(0, ZL, coulomb, 0)

    def got0(d, c):
        f = lax.rem(fft + d, NF)
        copy(cols, all_cols.at[f], sk.at[f], rk.at[f], band, f).wait_recv()
        return c

    lax.fori_loop(1, NF, got0, 0)
    lane_s = lax.broadcasted_iota(jnp.int32, (STP, L), 1).astype(F32)

    def ready(f, c):
        row_p[1:2, 0:STICKS] = all_cols[f].astype(F32)
        col = row_p[1:2, :]
        kx = jnp.floor((col + 0.5) * (1.0 / N))
        kx_of[f] = kx
        ky = jnp.transpose(jnp.broadcast_to(col - N * kx, (L, STP)))
        hot = jnp.where(lane_s == ky, 1.0, 0.0).astype(BF16)
        along_y[f] = dot(hot, hr[0:L]).astype(BF16)
        return c

    lax.fori_loop(0, NF, ready, 0)

    def got1(d, c):
        b = lax.rem(band + d, NBAND)
        copy(send1.at[b], recv1.at[b], s1.at[b], r1.at[b], b, fft).wait_recv()
        return c

    lax.fori_loop(1, NBAND, got1, 0)

    arrived = halves(recv1[...].reshape(NBAND * CAPP, L))
    picked = dot(sel[...], arrived)
    kept = keep[...] > 0.0
    hi = jnp.where(kept, picked[:, :L], 0.0).astype(BF16)
    lo = jnp.where(kept, picked[:, L:], 0.0).astype(BF16)
    along = fold(dot(jnp.concatenate([hi, lo], axis=1), hrz[...]))
    along = jnp.concatenate([along, jnp.zeros((STP - STICKS, L), F32)], axis=0)
    flipped = jnp.transpose(along)
    for f in range(NF):
        at_send[f] = flipped[f * ZP:(f + 1) * ZP]

    def go2(d, c):
        f = lax.rem(fft + d, NF)
        copy(at_send.at[f], at_recv.at[0, fft], s2.at[0, f], r2.at[0, fft], band, f).start()
        return c

    lax.fori_loop(1, NF, go2, 0)
    at_recv[0, fft] = at_send[fft]

    def go2n(d, c):
        f = lax.rem(fft + d, NF)
        copy(at_send.at[f], at_recv.at[1, fft], s2.at[1, f], r2.at[1, fft], prv, f).start()
        return c

    lax.fori_loop(0, NF, go2n, 0)

    def spread(which, f):
        kx = kx_of[f]
        a = at_recv[which, f]
        a_hi = a.astype(BF16).astype(F32)
        a_lo = a - a_hi
        w = [jnp.where(kx == x, part, 0.0).astype(BF16)
             for part in (a_hi, a_lo) for x in range(ZL)]
        g = fold(dot(jnp.concatenate(w, axis=0), along_y[f]))
        tb[f * BLK:(f + 1) * BLK, :] = g[:BLK] + g[BLK:]

    def stick_block(which, d, b, f):
        return copy(at_send.at[f], at_recv.at[which, f], s2.at[which, f], r2.at[which, f], b, f)

    def own_arrives(d, c):
        f = lax.rem(fft + d, NF)
        stick_block(0, d, band, f).wait_recv()
        return c

    def next_arrives(f, c):
        stick_block(1, f, nxt, f).wait_recv()
        return c

    def part(k, f):
        step, n = k // PARTS, k % PARTS
        p, first = step // 2, n * CHUNK
        src, dst, rsem = (send_b, recv_b, rb) if step % 2 else (send_f, recv_f, rf)
        return copy(src.at[p, f, first:first + CHUNK], dst.at[p, fft, first:first + CHUNK],
                    sp.at[k, f], rsem.at[p * PARTS + n, fft], band, f)

    def each_other(act):
        lax.fori_loop(1, NF, lambda d, c: (act(lax.rem(fft + d, NF)), c)[1], 0)

    def issue(k):
        if k >= 2:
            each_other(lambda f: part(k - 2, f).wait_send())
        each_other(lambda f: part(k, f).start())

    def arrived_parts(dst, rsem, p, n):
        first = n * CHUNK
        each_other(lambda f: copy(
            dst.at[p, f, first:first + CHUNK], dst.at[p, f, first:first + CHUNK],
            sp.at[0, f], rsem.at[p * PARTS + n, f], band, f).wait_recv())

    def density(p):
        for z in range(ZL):
            tb[pl.ds(z, L, stride=ZP), :] = left_mul(lx[...], phi[0, z] * phi[1 - p, z])

    def forward(p, n):
        first = n * CHUNK
        for f in range(NF):
            rows = f * BLK + first * ZP
            send_f[p, f, first:first + CHUNK] = right_mul(
                tb[rows:rows + CHUNK * ZP, :], hr[...]).reshape(CHUNK, ZP, L)
        recv_f[p, fft, first:first + CHUNK] = send_f[p, fft, first:first + CHUNK]

    def orbital(which, first, count):
        for z in range(first, first + count):
            phi[which, z] = left_mul(lx[...], tb[pl.ds(z, L, stride=ZP), :])

    def solve(p, n):
        arrived_parts(recv_f, rf, p, n)
        for x in range(n * CHUNK, (n + 1) * CHUNK):
            spec = left_mul(lz[...], recv_f[p, :, x].reshape(L, L)) * coul[x]
            send_b[p, :, x] = left_mul(lp[...], spec).reshape(NF, ZP, L)

    def backward(p):
        recv_b[p, fft] = send_b[p, fft]
        for n in range(PARTS):
            arrived_parts(recv_b, rb, p, n)
            for f in range(NF):
                rows = f * BLK + n * CHUNK * ZP
                tb2[rows:rows + CHUNK * ZP, :] = right_mul(
                    recv_b[p, f, n * CHUNK:(n + 1) * CHUNK].reshape(CHUNK * ZP, L), hr[...])

    lax.fori_loop(1, NF, own_arrives, 0)
    for f in range(NF):
        spread(0, f)
    orbital(0, 0, ZL)
    lax.fori_loop(0, NF, next_arrives, 0)
    for f in range(NF):
        spread(1, f)
    orbital(1, 0, ZL)
    density(0)
    for n in range(PARTS):
        forward(0, n)
        if n < 2:
            issue(n)
    density(1)
    for n in range(PARTS):
        forward(1, n)
    issue(2)
    for n in range(PARTS):
        solve(0, n)
        issue(3 + n)
    issue(6)
    issue(7)
    backward(0)
    far = lax.rem(band, 16) == 15
    nxt_row = (nxt // 16) * 16

    def to_next(first, count):
        return copy(send_v.at[pl.ds(first, count)], recv_v.at[pl.ds(first, count)],
                    sv, rv, nxt, fft)

    def to_relay(first, count, hop):
        return copy(send_v.at[pl.ds(first, count)], relay.at[pl.ds(0, count)],
                    sv, rr, nxt_row + 2 * hop, fft)

    def from_relay(first, count):
        return copy(relay.at[pl.ds(0, count)], recv_v.at[pl.ds(first, count)],
                    sr, rv, (band // 16) * 16, fft)

    def send_term(first, count, hop):
        if hop == 0:
            to_next(first, count).start()
        else:
            @pl.when(far)
            def _():
                to_relay(first, count, hop).start()

            @pl.when(jnp.logical_not(far))
            def _():
                to_next(first, count).start()

    for first, count, hop in ROUTES:
        for z in range(first, first + count):
            v = left_mul(lx[...], tb2[pl.ds(z, L, stride=ZP), :])
            acc[z] = (v * phi[1, z])[:N]
            send_v[z] = (v * phi[0, z])[:N]
        send_term(first, count, hop)
    issue(8)
    for n in range(PARTS):
        solve(1, n)
        issue(9 + n)
    for first, count, hop in ROUTES:
        if hop:
            @pl.when(lax.rem(band, 16) == 2 * hop)
            def _():
                to_relay(first, count, hop).wait_recv()
                from_relay(first, count).start()

    backward(1)
    for z in range(ZL):
        v = left_mul(lx[...], tb2[pl.ds(z, L, stride=ZP), :])
        acc[z] += (v * phi[0, z])[:N]
    to_next(0, ZL).wait_recv()
    for z in range(ZL):
        tb[pl.ds(z, N, stride=ZP), :] = acc[z] + recv_v[z]

    lane = lax.broadcasted_iota(jnp.int32, (ZP, L), 1)
    total = N * N
    for t in range(-(-total // L)):
        x, off = divmod(t * L, N)
        val = tb[x * ZP:(x + 1) * ZP, :]
        if off:
            val = pltpu.roll(val, L - off, 1)
        if x + 1 < N:
            more = pltpu.roll(tb[(x + 1) * ZP:(x + 2) * ZP, :], N - off, 1)
            val = jnp.where(lane < N - off, val, more)
        width = min(L, total - t * L)
        out[:, 0, t * L:t * L + width] = val[:ZL, :width]

    def left1(d, c):
        b = lax.rem(band + d, NBAND)
        copy(send1.at[b], recv1.at[b], s1.at[b], r1.at[b], b, fft).wait_send()
        return c

    lax.fori_loop(1, NBAND, left1, 0)

    def left2(d, c):
        f = lax.rem(fft + d, NF)
        copy(cols, all_cols.at[f], sk.at[f], rk.at[f], band, f).wait_send()
        stick_block(0, d, band, f).wait_send()
        for k in (10, 11):
            part(k, f).wait_send()
        return c

    lax.fori_loop(1, NF, left2, 0)

    def left2n(f, c):
        stick_block(1, f, prv, f).wait_send()
        return c

    lax.fori_loop(0, NF, left2n, 0)
    to_next(0, ZL).wait_send()
    for first, count, hop in ROUTES:
        if hop:
            @pl.when(lax.rem(band, 16) == 2 * hop)
            def _():
                from_relay(first, count).wait_send()


def local(coefficients, owned_sticks, stick_counts, stick_columns, band_order):
    tables = jnp.asarray(cas_parts())
    vmem = pl.BlockSpec(memory_space=pltpu.VMEM)
    dma = pltpu.SemaphoreType.DMA
    out = pl.pallas_call(
        kernel,
        out_shape=jax.ShapeDtypeStruct((ZL, 1, N * N), F32),
        in_specs=[pl.BlockSpec(memory_space=pltpu.HBM)] * 6,
        out_specs=vmem,
        scratch_shapes=[
            pltpu.VMEM((NBAND, CAP * N), F32),
            pltpu.VMEM((1, NBAND * CAP), jnp.int32),
            pltpu.VMEM((1, STICKS), jnp.int32),
            pltpu.VMEM((1, STICKS), jnp.int32),
            pltpu.SMEM((NBAND,), jnp.int32),
            pltpu.VMEM((7 * L, 2 * L), BF16),
            pltpu.VMEM((NBAND * CAPP, L), F32),
            pltpu.VMEM((NBAND, CAPP, L), F32),
            pltpu.VMEM((NBAND, CAPP, L), F32),
            pltpu.VMEM((NBAND, CAPP, L), F32),
            pltpu.VMEM((STICKS, NBAND * CAPP), BF16),
            pltpu.VMEM((STICKS, L), F32),
            pltpu.VMEM((1, NBAND * CAPP), jnp.int32),
            pltpu.VMEM((8, STP), F32),
            pltpu.VMEM((NF, 1, STICKS), jnp.int32),
            pltpu.VMEM((NF, 1, STP), F32),
            pltpu.VMEM((NF, STP, 2 * L), BF16),
            pltpu.VMEM((NF, ZP, STP), F32),
            pltpu.VMEM((2, NF, ZP, STP), F32),
            pltpu.VMEM((2, ZL, L, L), F32),
            pltpu.VMEM((L * ZP, L), F32),
            pltpu.VMEM((L * ZP, L), F32),
            pltpu.VMEM((ZL, L, L), F32),
            pltpu.VMEM((2, NF, ZL, ZP, L), F32),
            pltpu.VMEM((2, NF, ZL, ZP, L), F32),
            pltpu.VMEM((2, NF, ZL, ZP, L), F32),
            pltpu.VMEM((2, NF, ZL, ZP, L), F32),
            pltpu.VMEM((ZL, N, L), F32),
            pltpu.VMEM((ZL, N, L), F32),
            pltpu.VMEM((ZL, N, L), F32),
            pltpu.VMEM((4, N, L), F32),
            dma((NF,)), dma((NF,)),
            dma((NBAND,)), dma((NBAND,)),
            dma((2, NF)), dma((2, NF)),
            dma((4 * PARTS, NF)), dma((2 * PARTS, NF)), dma((2 * PARTS, NF)),
            dma, dma, dma, dma,
            dma((6,)),
        ],
        compiler_params=pltpu.CompilerParams(
            collective_id=0, has_side_effects=True, vmem_limit_bytes=48 * 1024 * 1024),
    )(*[pltpu.with_memory_space_constraint(a, pltpu.HBM) for a in (
        coefficients, owned_sticks, stick_counts, stick_columns, band_order, tables)])
    return out.reshape(1, ZL, N * N)


def solution(mesh):
    placed = (P(None, ("band", "fft")), P("fft", None), P("fft", None), P("fft", None), P())
    return jax.shard_map(
        local, mesh=mesh, in_specs=placed, out_specs=P("band", "fft", None), check_vma=False
    )
```

```python
import math

import jax
import jax.numpy as jnp
import ml_dtypes
import numpy as np
from jax import lax
from jax.experimental import pallas as pl
from jax.experimental.pallas import tpu as pltpu
from jax.sharding import PartitionSpec as P

N = 120
NF = 8
NBAND = 32
ZL = N // NF
ZP = 16
CAP = 22
CAPP = 24
STICKS = 352
STP = 384
L = 128
BLK = ZL * ZP
CHUNK = 5
PARTS = ZL // CHUNK
SEQUENCE = (
    [(1, 0, 0)]
    + [(0, 0, n) for n in range(PARTS)]
    + [(0, 1, n) for n in range(PARTS)]
    + [(1, 0, n) for n in range(1, PARTS)]
    + [(1, 1, n) for n in range(PARTS)]
)
ROUTES = ((0, 3, 6), (3, 3, 1), (6, 3, 5), (9, 2, 2), (11, 2, 7), (13, 2, 0))
COULOMB = 0.25
EXCHANGE_FRACTION = 0.25
F32 = jnp.float32
BF16 = jnp.bfloat16


def cas_parts():
    k = np.arange(N)
    angle = (k[:, None] * k[None, :] % N) * (2.0 * math.pi / N)
    full = np.cos(angle) + np.sin(angle)
    zpad = (k // ZL) * ZP + k % ZL

    def parts(a):
        hi = a.astype(ml_dtypes.bfloat16)
        lo = (a - hi.astype(np.float64)).astype(ml_dtypes.bfloat16)
        return hi, lo

    def place(rows, cols):
        out = np.zeros((L, L))
        out[np.ix_(rows, cols)] = full
        return out

    def right(a):
        hi, lo = parts(a)
        row = np.concatenate([hi, lo], axis=1)
        return np.concatenate([row, row], axis=0)

    def left(a):
        hi, lo = parts(a)
        return np.concatenate([hi, lo], axis=1)

    plain = place(k, k)
    return np.concatenate([
        right(plain),
        right(place(k, zpad)),
        left(plain),
        left(place(zpad, k)),
        left(place(k, zpad)),
    ], axis=0)


def halves(x):
    hi = x.astype(BF16)
    lo = (x - hi.astype(F32)).astype(BF16)
    return jnp.concatenate([hi, lo], axis=1)


def fold(r):
    return r[:, :L] + r[:, L:]


def dot(a, b):
    return jnp.dot(a, b, preferred_element_type=F32)


def right_mul(x, table):
    return fold(dot(halves(x), table))


def left_mul(table, x):
    cat = halves(x)
    return fold(dot(table, jnp.concatenate([cat, cat], axis=0)))


def kernel(
    coef_h, owned_h, counts_h, cols_h, order_h, tables_h, out,
    coef, owned, counts, cols, order, tables,
    stage, stage3, send1, recv1, sel, keep, owned_p, row_p, all_cols, kx_of, along_y, at_send, at_recv, phi, tb, tb2,
    coul, send_f, recv_f, send_b, recv_b, send_v, recv_v, acc, relay,
    sk, rk, s1, r1, s2, r2, sp, rf, rb, sv, rv, rr, sr, sin,
):
    hr = tables.at[0:2 * L]
    hrz = tables.at[2 * L:4 * L]
    lx = tables.at[4 * L:5 * L]
    lp = tables.at[5 * L:6 * L]
    lz = tables.at[6 * L:7 * L]
    band = lax.axis_index("band")
    fft = lax.axis_index("fft")
    nxt = lax.rem(band + 1, NBAND)
    prv = lax.rem(band + NBAND - 1, NBAND)

    def copy(src, dst, ssem, rsem, b, f):
        return pltpu.make_async_remote_copy(
            src_ref=src, dst_ref=dst, send_sem=ssem, recv_sem=rsem,
            device_id=(b, f), device_id_type=pl.DeviceIdType.MESH,
        )

    loads = [
        pltpu.make_async_copy(src, dst, sin.at[n])
        for n, (src, dst) in enumerate([
            (coef_h, coef), (order_h, order), (owned_h, owned), (counts_h, counts),
            (cols_h, cols), (tables_h, tables)])
    ]
    loads[0].start()
    loads[1].start()

    barrier = pltpu.get_barrier_semaphore()

    def hello_band(d, c):
        pl.semaphore_signal(
            barrier, inc=1, device_id=(lax.rem(band + d, NBAND), fft),
            device_id_type=pl.DeviceIdType.MESH)
        return c

    lax.fori_loop(1, NBAND, hello_band, 0)

    def hello_fft(d, c):
        f = lax.rem(fft + d, NF)
        pl.semaphore_signal(
            barrier, inc=1, device_id=(band, f), device_id_type=pl.DeviceIdType.MESH)
        pl.semaphore_signal(
            barrier, inc=1, device_id=(nxt, f), device_id_type=pl.DeviceIdType.MESH)
        return c

    lax.fori_loop(1, NF, hello_fft, 0)

    for load in loads[2:]:
        load.start()

    stage[...] = jnp.zeros(stage.shape, F32)
    loads[0].wait()
    for q in range(CAP):
        stage[pl.ds(q, NBAND, stride=CAPP), pl.ds(0, N)] = coef[:, N * q:N * q + N]

    stage3[...] = stage[...].reshape(NBAND, CAPP, L)

    loads[1].wait()

    def reorder(j, c):
        send1[j] = stage3[order[j]][:CAP]
        return c

    lax.fori_loop(0, NBAND, reorder, 0)

    pl.semaphore_wait(barrier, NBAND - 1 + 2 * (NF - 1))

    loads[4].wait()
    all_cols[fft] = cols[...]

    def go0(d, c):
        f = lax.rem(fft + d, NF)
        copy(cols, all_cols.at[fft], sk.at[f], rk.at[fft], band, f).start()
        return c

    lax.fori_loop(1, NF, go0, 0)

    for d in sorted(range(1, NBAND), key=lambda d: (abs(d % 16 - 8), d)):
        b = lax.rem(band + d, NBAND)
        copy(send1.at[b], recv1.at[band], s1.at[b], r1.at[band], b, fft).start()
    recv1[band] = send1[band]

    tb[...] = jnp.zeros(tb.shape, F32)
    recv_f[...] = jnp.zeros(recv_f.shape, F32)
    recv_b[...] = jnp.zeros(recv_b.shape, F32)
    tb2[N * ZP:, :] = jnp.zeros(((L - N) * ZP, L), F32)
    for n in (2, 3, 5):
        loads[n].wait()
    owned_p[...] = jnp.full(owned_p.shape, -1, jnp.int32)
    for o in range(NBAND):
        owned_p[:, CAPP * o:CAPP * o + CAP] = owned[:, CAP * o:CAP * o + CAP]
    rows = lax.broadcasted_iota(jnp.int32, (STICKS, NBAND * CAPP), 0)
    sel[...] = jnp.where(rows == owned_p[...], 1.0, 0.0).astype(BF16)
    row_p[...] = jnp.full(row_p.shape, -1.0, F32)
    row_p[0:1, 0:STICKS] = counts[...].astype(F32)
    count_b = jnp.transpose(jnp.broadcast_to(row_p[0:1, :], (L, STP)))[:STICKS]
    kz = lax.broadcasted_iota(jnp.int32, (STICKS, L), 1)
    need = (2 * jnp.minimum(kz, N - kz) + 1).astype(F32)
    keep[...] = jnp.where((kz < N) & (need <= count_b), 1.0, 0.0)
    scale = -EXCHANGE_FRACTION * COULOMB * math.sqrt(N ** 3) / N ** 3
    r0 = lax.broadcasted_iota(jnp.int32, (L, L), 0)
    r1_ = lax.broadcasted_iota(jnp.int32, (L, L), 1)
    mz = jnp.minimum(r0, N - r0)
    my = jnp.minimum(r1_, N - r1_)
    plane = mz * mz + my * my

    def coulomb(x, c):
        kx = fft * ZL + x
        mx = jnp.minimum(kx, N - kx)
        q = (plane + mx * mx).astype(F32)
        coul[x] = jnp.where(q > 0.0, scale / jnp.maximum(q, 1.0), 0.0)
        return c

    lax.fori_loop(0, ZL, coulomb, 0)

    def got0(d, c):
        f = lax.rem(fft + d, NF)
        copy(cols, all_cols.at[f], sk.at[f], rk.at[f], band, f).wait_recv()
        return c

    lax.fori_loop(1, NF, got0, 0)
    lane_s = lax.broadcasted_iota(jnp.int32, (STP, L), 1).astype(F32)

    def ready(f, c):
        row_p[1:2, 0:STICKS] = all_cols[f].astype(F32)
        col = row_p[1:2, :]
        kx = jnp.floor((col + 0.5) * (1.0 / N))
        kx_of[f] = kx
        ky = jnp.transpose(jnp.broadcast_to(col - N * kx, (L, STP)))
        hot = jnp.where(lane_s == ky, 1.0, 0.0).astype(BF16)
        along_y[f] = dot(hot, hr[0:L]).astype(BF16)
        return c

    lax.fori_loop(0, NF, ready, 0)

    def got1(d, c):
        b = lax.rem(band + d, NBAND)
        copy(send1.at[b], recv1.at[b], s1.at[b], r1.at[b], b, fft).wait_recv()
        return c

    lax.fori_loop(1, NBAND, got1, 0)

    stage3[:, 0:CAP, :] = recv1[...]
    arrived = halves(stage3[...].reshape(NBAND * CAPP, L))
    picked = dot(sel[...], arrived)
    kept = keep[...] > 0.0
    hi = jnp.where(kept, picked[:, :L], 0.0).astype(BF16)
    lo = jnp.where(kept, picked[:, L:], 0.0).astype(BF16)
    along = fold(dot(jnp.concatenate([hi, lo], axis=1), hrz[...]))
    along = jnp.concatenate([along, jnp.zeros((STP - STICKS, L), F32)], axis=0)
    flipped = jnp.transpose(along)
    for f in range(NF):
        at_send[f] = flipped[f * ZP:(f + 1) * ZP]

    def go2(d, c):
        f = lax.rem(fft + d, NF)
        copy(at_send.at[f], at_recv.at[0, fft], s2.at[0, f], r2.at[0, fft], band, f).start()
        return c

    lax.fori_loop(1, NF, go2, 0)
    at_recv[0, fft] = at_send[fft]

    def go2n(d, c):
        f = lax.rem(fft + d, NF)
        copy(at_send.at[f], at_recv.at[1, fft], s2.at[1, f], r2.at[1, fft], prv, f).start()
        return c

    lax.fori_loop(0, NF, go2n, 0)

    def spread(which, f):
        kx = kx_of[f]
        a = at_recv[which, f]
        a_hi = a.astype(BF16).astype(F32)
        a_lo = a - a_hi
        w = [jnp.where(kx == x, part, 0.0).astype(BF16)
             for part in (a_hi, a_lo) for x in range(ZL)]
        g = fold(dot(jnp.concatenate(w, axis=0), along_y[f]))
        tb[f * BLK:(f + 1) * BLK, :] = g[:BLK] + g[BLK:]

    def stick_block(which, d, b, f):
        return copy(at_send.at[f], at_recv.at[which, f], s2.at[which, f], r2.at[which, f], b, f)

    def own_arrives(d, c):
        f = lax.rem(fft + d, NF)
        stick_block(0, d, band, f).wait_recv()
        return c

    def next_arrives(f, c):
        stick_block(1, f, nxt, f).wait_recv()
        return c

    def part(k, f):
        p, back, n = SEQUENCE[k]
        first = n * CHUNK
        src, dst, rsem = (send_b, recv_b, rb) if back else (send_f, recv_f, rf)
        return copy(src.at[p, f, first:first + CHUNK, 0:ZL],
                    dst.at[p, fft, first:first + CHUNK, 0:ZL],
                    sp.at[k, f], rsem.at[p * PARTS + n, fft], band, f)

    def each_other(act):
        lax.fori_loop(1, NF, lambda d, c: (act(lax.rem(fft + d, NF)), c)[1], 0)

    def issue(k):
        if k >= 2:
            each_other(lambda f: part(k - 2, f).wait_send())
        each_other(lambda f: part(k, f).start())

    def arrived_parts(dst, rsem, p, n):
        first = n * CHUNK
        each_other(lambda f: copy(
            dst.at[p, f, first:first + CHUNK, 0:ZL],
            dst.at[p, f, first:first + CHUNK, 0:ZL],
            sp.at[0, f], rsem.at[p * PARTS + n, f], band, f).wait_recv())

    def density(p):
        for z in range(ZL):
            tb[pl.ds(z, L, stride=ZP), :] = left_mul(lx[...], phi[0, z] * phi[1 - p, z])

    def forward(p, n):
        first = n * CHUNK
        for f in range(NF):
            rows = f * BLK + first * ZP
            send_f[p, f, first:first + CHUNK] = right_mul(
                tb[rows:rows + CHUNK * ZP, :], hr[...]).reshape(CHUNK, ZP, L)
        recv_f[p, fft, first:first + CHUNK] = send_f[p, fft, first:first + CHUNK]

    def orbital(which, first, count):
        for z in range(first, first + count):
            phi[which, z] = left_mul(lx[...], tb[pl.ds(z, L, stride=ZP), :])

    def solve(p, n):
        arrived_parts(recv_f, rf, p, n)
        for x in range(n * CHUNK, (n + 1) * CHUNK):
            spec = left_mul(lz[...], recv_f[p, :, x].reshape(L, L)) * coul[x]
            send_b[p, :, x] = left_mul(lp[...], spec).reshape(NF, ZP, L)

    def backward(p):
        recv_b[p, fft] = send_b[p, fft]
        for n in range(PARTS):
            arrived_parts(recv_b, rb, p, n)
            for f in range(NF):
                rows = f * BLK + n * CHUNK * ZP
                tb2[rows:rows + CHUNK * ZP, :] = right_mul(
                    recv_b[p, f, n * CHUNK:(n + 1) * CHUNK].reshape(CHUNK * ZP, L), hr[...])

    lax.fori_loop(1, NF, own_arrives, 0)
    for f in range(NF):
        spread(0, f)
    orbital(0, 0, ZL)
    density(1)
    forward(1, 0)
    issue(0)
    for n in range(1, PARTS):
        forward(1, n)
    lax.fori_loop(0, NF, next_arrives, 0)
    for f in range(NF):
        spread(1, f)
    orbital(1, 0, ZL)
    density(0)
    for n in range(PARTS):
        forward(0, n)
        issue(1 + n)
    for n in range(PARTS):
        solve(0, n)
        issue(1 + PARTS + n)
    for n in range(1, PARTS):
        issue(2 * PARTS + n)
    backward(0)
    far = lax.rem(band, 16) == 15
    nxt_row = (nxt // 16) * 16

    def to_next(first, count):
        return copy(send_v.at[pl.ds(first, count)], recv_v.at[pl.ds(first, count)],
                    sv, rv, nxt, fft)

    def to_relay(first, count, hop):
        return copy(send_v.at[pl.ds(first, count)], relay.at[pl.ds(0, count)],
                    sv, rr, nxt_row + 2 * hop, fft)

    def from_relay(first, count):
        return copy(relay.at[pl.ds(0, count)], recv_v.at[pl.ds(first, count)],
                    sr, rv, (band // 16) * 16, fft)

    def send_term(first, count, hop):
        if hop == 0:
            to_next(first, count).start()
        else:
            @pl.when(far)
            def _():
                to_relay(first, count, hop).start()

            @pl.when(jnp.logical_not(far))
            def _():
                to_next(first, count).start()

    for first, count, hop in ROUTES:
        for z in range(first, first + count):
            v = left_mul(lx[...], tb2[pl.ds(z, L, stride=ZP), :])
            acc[z] = (v * phi[1, z])[:N]
            send_v[z] = (v * phi[0, z])[:N]
        send_term(first, count, hop)
    for n in range(PARTS):
        solve(1, n)
        issue(3 * PARTS + n)
    for first, count, hop in ROUTES:
        if hop:
            @pl.when(lax.rem(band, 16) == 2 * hop)
            def _():
                to_relay(first, count, hop).wait_recv()
                from_relay(first, count).start()

    backward(1)
    for z in range(ZL):
        v = left_mul(lx[...], tb2[pl.ds(z, L, stride=ZP), :])
        acc[z] += (v * phi[0, z])[:N]
    to_next(0, ZL).wait_recv()
    for z in range(ZL):
        tb[pl.ds(z, N, stride=ZP), :] = acc[z] + recv_v[z]

    lane = lax.broadcasted_iota(jnp.int32, (ZP, L), 1)
    total = N * N
    for t in range(-(-total // L)):
        x, off = divmod(t * L, N)
        val = tb[x * ZP:(x + 1) * ZP, :]
        if off:
            val = pltpu.roll(val, L - off, 1)
        if x + 1 < N:
            more = pltpu.roll(tb[(x + 1) * ZP:(x + 2) * ZP, :], N - off, 1)
            val = jnp.where(lane < N - off, val, more)
        width = min(L, total - t * L)
        out[:, 0, t * L:t * L + width] = val[:ZL, :width]

    def left1(d, c):
        b = lax.rem(band + d, NBAND)
        copy(send1.at[b], recv1.at[b], s1.at[b], r1.at[b], b, fft).wait_send()
        return c

    lax.fori_loop(1, NBAND, left1, 0)

    def left2(d, c):
        f = lax.rem(fft + d, NF)
        copy(cols, all_cols.at[f], sk.at[f], rk.at[f], band, f).wait_send()
        stick_block(0, d, band, f).wait_send()
        for k in (4 * PARTS - 2, 4 * PARTS - 1):
            part(k, f).wait_send()
        return c

    lax.fori_loop(1, NF, left2, 0)

    def left2n(f, c):
        stick_block(1, f, prv, f).wait_send()
        return c

    lax.fori_loop(0, NF, left2n, 0)
    to_next(0, ZL).wait_send()
    for first, count, hop in ROUTES:
        if hop:
            @pl.when(lax.rem(band, 16) == 2 * hop)
            def _():
                from_relay(first, count).wait_send()


def local(coefficients, owned_sticks, stick_counts, stick_columns, band_order):
    tables = jnp.asarray(cas_parts())
    vmem = pl.BlockSpec(memory_space=pltpu.VMEM)
    dma = pltpu.SemaphoreType.DMA
    out = pl.pallas_call(
        kernel,
        out_shape=jax.ShapeDtypeStruct((ZL, 1, N * N), F32),
        in_specs=[pl.BlockSpec(memory_space=pltpu.HBM)] * 6,
        out_specs=vmem,
        scratch_shapes=[
            pltpu.VMEM((NBAND, CAP * N), F32),
            pltpu.VMEM((1, NBAND * CAP), jnp.int32),
            pltpu.VMEM((1, STICKS), jnp.int32),
            pltpu.VMEM((1, STICKS), jnp.int32),
            pltpu.SMEM((NBAND,), jnp.int32),
            pltpu.VMEM((7 * L, 2 * L), BF16),
            pltpu.VMEM((NBAND * CAPP, L), F32),
            pltpu.VMEM((NBAND, CAPP, L), F32),
            pltpu.VMEM((NBAND, CAP, L), F32),
            pltpu.VMEM((NBAND, CAP, L), F32),
            pltpu.VMEM((STICKS, NBAND * CAPP), BF16),
            pltpu.VMEM((STICKS, L), F32),
            pltpu.VMEM((1, NBAND * CAPP), jnp.int32),
            pltpu.VMEM((8, STP), F32),
            pltpu.VMEM((NF, 1, STICKS), jnp.int32),
            pltpu.VMEM((NF, 1, STP), F32),
            pltpu.VMEM((NF, STP, 2 * L), BF16),
            pltpu.VMEM((NF, ZP, STP), F32),
            pltpu.VMEM((2, NF, ZP, STP), F32),
            pltpu.VMEM((2, ZL, L, L), F32),
            pltpu.VMEM((L * ZP, L), F32),
            pltpu.VMEM((L * ZP, L), F32),
            pltpu.VMEM((ZL, L, L), F32),
            pltpu.VMEM((2, NF, ZL, ZP, L), F32),
            pltpu.VMEM((2, NF, ZL, ZP, L), F32),
            pltpu.VMEM((2, NF, ZL, ZP, L), F32),
            pltpu.VMEM((2, NF, ZL, ZP, L), F32),
            pltpu.VMEM((ZL, N, L), F32),
            pltpu.VMEM((ZL, N, L), F32),
            pltpu.VMEM((ZL, N, L), F32),
            pltpu.VMEM((4, N, L), F32),
            dma((NF,)), dma((NF,)),
            dma((NBAND,)), dma((NBAND,)),
            dma((2, NF)), dma((2, NF)),
            dma((4 * PARTS, NF)), dma((2 * PARTS, NF)), dma((2 * PARTS, NF)),
            dma, dma, dma, dma,
            dma((6,)),
        ],
        compiler_params=pltpu.CompilerParams(
            collective_id=0, has_side_effects=True, vmem_limit_bytes=48 * 1024 * 1024),
    )(*[pltpu.with_memory_space_constraint(a, pltpu.HBM) for a in (
        coefficients, owned_sticks, stick_counts, stick_columns, band_order, tables)])
    return out.reshape(1, ZL, N * N)


def solution(mesh):
    placed = (P(None, ("band", "fft")), P("fft", None), P("fft", None), P("fft", None), P())
    return jax.shard_map(
        local, mesh=mesh, in_specs=placed, out_specs=P("band", "fft", None), check_vma=False
    )
```

```python
import math

import jax
import jax.numpy as jnp
import ml_dtypes
import numpy as np
from jax import lax
from jax.experimental import pallas as pl
from jax.experimental.pallas import tpu as pltpu
from jax.sharding import PartitionSpec as P

N = 120
NF = 8
NBAND = 32
ZL = N // NF
ZP = 16
CAP = 22
CAPP = 24
STICKS = 352
STP = 384
L = 128
BLK = ZL * ZP
CHUNK = 5
PARTS = ZL // CHUNK
SEQUENCE = (
    [(1, 0, 0)]
    + [(0, 0, n) for n in range(PARTS)]
    + [(0, 1, n) for n in range(PARTS)]
    + [(1, 0, n) for n in range(1, PARTS)]
    + [(1, 1, n) for n in range(PARTS)]
)
ROUTES = ((0, 3, 6), (3, 3, 1), (6, 3, 5), (9, 2, 2), (11, 2, 7), (13, 2, 0))
COULOMB = 0.25
EXCHANGE_FRACTION = 0.25
F32 = jnp.float32
BF16 = jnp.bfloat16


def cas_parts():
    k = np.arange(N)
    angle = (k[:, None] * k[None, :] % N) * (2.0 * math.pi / N)
    full = np.cos(angle) + np.sin(angle)
    zpad = (k // ZL) * ZP + k % ZL

    def parts(a):
        hi = a.astype(ml_dtypes.bfloat16)
        lo = (a - hi.astype(np.float64)).astype(ml_dtypes.bfloat16)
        return hi, lo

    def place(rows, cols):
        out = np.zeros((L, L))
        out[np.ix_(rows, cols)] = full
        return out

    def right(a):
        hi, lo = parts(a)
        row = np.concatenate([hi, lo], axis=1)
        return np.concatenate([row, row], axis=0)

    def left(a):
        hi, lo = parts(a)
        return np.concatenate([hi, lo], axis=1)

    plain = place(k, k)
    return np.concatenate([
        right(plain),
        right(place(k, zpad)),
        left(plain),
        left(place(zpad, k)),
        left(place(k, zpad)),
    ], axis=0)


def halves(x):
    hi = x.astype(BF16)
    lo = (x - hi.astype(F32)).astype(BF16)
    return jnp.concatenate([hi, lo], axis=1)


def fold(r):
    return r[:, :L] + r[:, L:]


def dot(a, b):
    return jnp.dot(a, b, preferred_element_type=F32)


def right_mul(x, table):
    return fold(dot(halves(x), table))


def left_mul(table, x):
    cat = halves(x)
    return fold(dot(table, jnp.concatenate([cat, cat], axis=0)))


def kernel(
    coef_h, owned_h, counts_h, cols_h, order_h, tables_h, out,
    coef, owned, counts, cols, order, tables,
    stage, stage3, send1, recv1, sel, keep, owned_p, row_p, all_cols, kx_of, along_y, at_send, at_recv, phi, tb, tb2,
    coul, send_f, recv_f, send_b, recv_b, send_v, recv_v, acc, relay,
    sk, rk, s1, r1, s2, r2, sp, rf, rb, sv, rv, rr, sr, sin,
):
    hr = tables.at[0:2 * L]
    hrz = tables.at[2 * L:4 * L]
    lx = tables.at[4 * L:5 * L]
    lp = tables.at[5 * L:6 * L]
    lz = tables.at[6 * L:7 * L]
    band = lax.axis_index("band")
    fft = lax.axis_index("fft")
    nxt = lax.rem(band + 1, NBAND)
    prv = lax.rem(band + NBAND - 1, NBAND)

    def copy(src, dst, ssem, rsem, b, f):
        return pltpu.make_async_remote_copy(
            src_ref=src, dst_ref=dst, send_sem=ssem, recv_sem=rsem,
            device_id=(b, f), device_id_type=pl.DeviceIdType.MESH,
        )

    loads = [
        pltpu.make_async_copy(src, dst, sin.at[n])
        for n, (src, dst) in enumerate([
            (coef_h, coef), (order_h, order), (owned_h, owned), (counts_h, counts),
            (cols_h, cols), (tables_h, tables)])
    ]
    loads[0].start()
    loads[1].start()

    barrier = pltpu.get_barrier_semaphore()

    def hello_band(d, c):
        pl.semaphore_signal(
            barrier, inc=1, device_id=(lax.rem(band + d, NBAND), fft),
            device_id_type=pl.DeviceIdType.MESH)
        return c

    lax.fori_loop(1, NBAND, hello_band, 0)

    def hello_fft(d, c):
        f = lax.rem(fft + d, NF)
        pl.semaphore_signal(
            barrier, inc=1, device_id=(band, f), device_id_type=pl.DeviceIdType.MESH)
        pl.semaphore_signal(
            barrier, inc=1, device_id=(nxt, f), device_id_type=pl.DeviceIdType.MESH)
        return c

    lax.fori_loop(1, NF, hello_fft, 0)

    for load in loads[2:]:
        load.start()

    stage[...] = jnp.zeros(stage.shape, F32)
    loads[0].wait()
    for q in range(CAP):
        stage[pl.ds(q, NBAND, stride=CAPP), pl.ds(0, N)] = coef[:, N * q:N * q + N]

    stage3[...] = stage[...].reshape(NBAND, CAPP, L)

    loads[1].wait()

    def reorder(j, c):
        send1[j] = stage3[order[j]][:CAP]
        return c

    lax.fori_loop(0, NBAND, reorder, 0)

    pl.semaphore_wait(barrier, NBAND - 1 + 2 * (NF - 1))

    loads[4].wait()
    all_cols[fft] = cols[...]

    def go0(d, c):
        f = lax.rem(fft + d, NF)
        copy(cols, all_cols.at[fft], sk.at[f], rk.at[fft], band, f).start()
        return c

    lax.fori_loop(1, NF, go0, 0)

    for d in sorted(range(1, NBAND), key=lambda d: (abs(d % 16 - 8), d)):
        b = lax.rem(band + d, NBAND)
        copy(send1.at[b], recv1.at[band], s1.at[b], r1.at[band], b, fft).start()
    recv1[band] = send1[band]

    tb[...] = jnp.zeros(tb.shape, F32)
    recv_f[...] = jnp.zeros(recv_f.shape, F32)
    recv_b[...] = jnp.zeros(recv_b.shape, F32)
    tb2[N * ZP:, :] = jnp.zeros(((L - N) * ZP, L), F32)
    for n in (2, 3, 5):
        loads[n].wait()
    owned_p[...] = jnp.full(owned_p.shape, -1, jnp.int32)
    for o in range(NBAND):
        owned_p[:, CAPP * o:CAPP * o + CAP] = owned[:, CAP * o:CAP * o + CAP]
    rows = lax.broadcasted_iota(jnp.int32, (STICKS, NBAND * CAPP), 0)
    sel[...] = jnp.where(rows == owned_p[...], 1.0, 0.0).astype(BF16)
    row_p[...] = jnp.full(row_p.shape, -1.0, F32)
    row_p[0:1, 0:STICKS] = counts[...].astype(F32)
    count_b = jnp.transpose(jnp.broadcast_to(row_p[0:1, :], (L, STP)))[:STICKS]
    kz = lax.broadcasted_iota(jnp.int32, (STICKS, L), 1)
    need = (2 * jnp.minimum(kz, N - kz) + 1).astype(F32)
    keep[...] = jnp.where((kz < N) & (need <= count_b), 1.0, 0.0)
    scale = -EXCHANGE_FRACTION * COULOMB * math.sqrt(N ** 3) / N ** 3
    r0 = lax.broadcasted_iota(jnp.int32, (L, L), 0)
    r1_ = lax.broadcasted_iota(jnp.int32, (L, L), 1)
    mz = jnp.minimum(r0, N - r0)
    my = jnp.minimum(r1_, N - r1_)
    plane = mz * mz + my * my

    def coulomb(x, c):
        kx = fft * ZL + x
        mx = jnp.minimum(kx, N - kx)
        q = (plane + mx * mx).astype(F32)
        coul[x] = jnp.where(q > 0.0, scale / jnp.maximum(q, 1.0), 0.0)
        return c

    lax.fori_loop(0, ZL, coulomb, 0)

    def got0(d, c):
        f = lax.rem(fft + d, NF)
        copy(cols, all_cols.at[f], sk.at[f], rk.at[f], band, f).wait_recv()
        return c

    lax.fori_loop(1, NF, got0, 0)
    lane_s = lax.broadcasted_iota(jnp.int32, (STP, L), 1).astype(F32)

    def ready(f, c):
        row_p[1:2, 0:STICKS] = all_cols[f].astype(F32)
        col = row_p[1:2, :]
        kx = jnp.floor((col + 0.5) * (1.0 / N))
        kx_of[f] = kx
        ky = jnp.transpose(jnp.broadcast_to(col - N * kx, (L, STP)))
        hot = jnp.where(lane_s == ky, 1.0, 0.0).astype(BF16)
        along_y[f] = dot(hot, hr[0:L]).astype(BF16)
        return c

    lax.fori_loop(0, NF, ready, 0)

    def got1(d, c):
        b = lax.rem(band + d, NBAND)
        copy(send1.at[b], recv1.at[b], s1.at[b], r1.at[b], b, fft).wait_recv()
        return c

    lax.fori_loop(1, NBAND, got1, 0)

    stage3[:, 0:CAP, :] = recv1[...]
    arrived = halves(stage3[...].reshape(NBAND * CAPP, L))
    picked = dot(sel[...], arrived)
    kept = keep[...] > 0.0
    hi = jnp.where(kept, picked[:, :L], 0.0).astype(BF16)
    lo = jnp.where(kept, picked[:, L:], 0.0).astype(BF16)
    along = fold(dot(jnp.concatenate([hi, lo], axis=1), hrz[...]))
    along = jnp.concatenate([along, jnp.zeros((STP - STICKS, L), F32)], axis=0)
    flipped = jnp.transpose(along)
    for f in range(NF):
        at_send[f] = flipped[f * ZP:(f + 1) * ZP]

    def go2(d, c):
        f = lax.rem(fft + d, NF)
        copy(at_send.at[f], at_recv.at[0, fft], s2.at[0, f], r2.at[0, fft], band, f).start()
        return c

    lax.fori_loop(1, NF, go2, 0)
    at_recv[0, fft] = at_send[fft]

    def go2n(d, c):
        f = lax.rem(fft + d, NF)
        copy(at_send.at[f], at_recv.at[1, fft], s2.at[1, f], r2.at[1, fft], prv, f).start()
        return c

    lax.fori_loop(0, NF, go2n, 0)

    def spread(which, f):
        kx = kx_of[f]
        a = at_recv[which, f]
        a_hi = a.astype(BF16).astype(F32)
        a_lo = a - a_hi
        w = [jnp.where(kx == x, part, 0.0).astype(BF16)
             for part in (a_hi, a_lo) for x in range(ZL)]
        g = fold(dot(jnp.concatenate(w, axis=0), along_y[f]))
        tb[f * BLK:(f + 1) * BLK, :] = g[:BLK] + g[BLK:]

    def stick_block(which, d, b, f):
        return copy(at_send.at[f], at_recv.at[which, f], s2.at[which, f], r2.at[which, f], b, f)

    def own_arrives(d, c):
        f = lax.rem(fft + d, NF)
        stick_block(0, d, band, f).wait_recv()
        return c

    def next_arrives(f, c):
        stick_block(1, f, nxt, f).wait_recv()
        return c

    def part(k, f):
        p, back, n = SEQUENCE[k]
        first = n * CHUNK
        src, dst, rsem = (send_b, recv_b, rb) if back else (send_f, recv_f, rf)
        return copy(src.at[p, f, first:first + CHUNK, 0:ZL],
                    dst.at[p, fft, first:first + CHUNK, 0:ZL],
                    sp.at[k, f], rsem.at[p * PARTS + n, fft], band, f)

    def each_other(act):
        lax.fori_loop(1, NF, lambda d, c: (act(lax.rem(fft + d, NF)), c)[1], 0)

    def issue(k):
        if k >= 3:
            each_other(lambda f: part(k - 3, f).wait_send())
        each_other(lambda f: part(k, f).start())

    def arrived_parts(dst, rsem, p, n):
        first = n * CHUNK
        each_other(lambda f: copy(
            dst.at[p, f, first:first + CHUNK, 0:ZL],
            dst.at[p, f, first:first + CHUNK, 0:ZL],
            sp.at[0, f], rsem.at[p * PARTS + n, f], band, f).wait_recv())

    def density(p):
        for z in range(ZL):
            tb[pl.ds(z, L, stride=ZP), :] = left_mul(lx[...], phi[0, z] * phi[1 - p, z])

    def forward(p, n):
        first = n * CHUNK
        for f in range(NF):
            rows = f * BLK + first * ZP
            send_f[p, f, first:first + CHUNK] = right_mul(
                tb[rows:rows + CHUNK * ZP, :], hr[...]).reshape(CHUNK, ZP, L)
        recv_f[p, fft, first:first + CHUNK] = send_f[p, fft, first:first + CHUNK]

    def orbital(which, first, count):
        for z in range(first, first + count):
            phi[which, z] = left_mul(lx[...], tb[pl.ds(z, L, stride=ZP), :])

    def solve(p, n):
        arrived_parts(recv_f, rf, p, n)
        for x in range(n * CHUNK, (n + 1) * CHUNK):
            spec = left_mul(lz[...], recv_f[p, :, x].reshape(L, L)) * coul[x]
            send_b[p, :, x] = left_mul(lp[...], spec).reshape(NF, ZP, L)

    def backward(p):
        recv_b[p, fft] = send_b[p, fft]
        for n in range(PARTS):
            arrived_parts(recv_b, rb, p, n)
            for f in range(NF):
                rows = f * BLK + n * CHUNK * ZP
                tb2[rows:rows + CHUNK * ZP, :] = right_mul(
                    recv_b[p, f, n * CHUNK:(n + 1) * CHUNK].reshape(CHUNK * ZP, L), hr[...])

    lax.fori_loop(1, NF, own_arrives, 0)
    for f in range(NF):
        spread(0, f)
    orbital(0, 0, ZL)
    density(1)
    forward(1, 0)
    issue(0)
    for n in range(1, PARTS):
        forward(1, n)
    lax.fori_loop(0, NF, next_arrives, 0)
    for f in range(NF):
        spread(1, f)
    orbital(1, 0, ZL)
    density(0)
    for n in range(PARTS):
        forward(0, n)
        issue(1 + n)
    for n in range(PARTS):
        solve(0, n)
        issue(1 + PARTS + n)
    for n in range(1, PARTS):
        issue(2 * PARTS + n)
    backward(0)
    far = lax.rem(band, 16) == 15
    nxt_row = (nxt // 16) * 16

    def to_next(first, count):
        return copy(send_v.at[pl.ds(first, count)], recv_v.at[pl.ds(first, count)],
                    sv, rv, nxt, fft)

    def to_relay(first, count, hop):
        return copy(send_v.at[pl.ds(first, count)], relay.at[pl.ds(0, count)],
                    sv, rr, nxt_row + 2 * hop, fft)

    def from_relay(first, count):
        return copy(relay.at[pl.ds(0, count)], recv_v.at[pl.ds(first, count)],
                    sr, rv, (band // 16) * 16, fft)

    def send_term(first, count, hop):
        if hop == 0:
            to_next(first, count).start()
        else:
            @pl.when(far)
            def _():
                to_relay(first, count, hop).start()

            @pl.when(jnp.logical_not(far))
            def _():
                to_next(first, count).start()

    for first, count, hop in ROUTES:
        for z in range(first, first + count):
            v = left_mul(lx[...], tb2[pl.ds(z, L, stride=ZP), :])
            acc[z] = (v * phi[1, z])[:N]
            send_v[z] = (v * phi[0, z])[:N]
        send_term(first, count, hop)
    for n in range(PARTS):
        solve(1, n)
        issue(3 * PARTS + n)
    for first, count, hop in ROUTES:
        if hop:
            @pl.when(lax.rem(band, 16) == 2 * hop)
            def _():
                to_relay(first, count, hop).wait_recv()
                from_relay(first, count).start()

    backward(1)
    to_next(0, ZL).wait_recv()
    for z in range(ZL):
        v = left_mul(lx[...], tb2[pl.ds(z, L, stride=ZP), :])
        tb[pl.ds(z, N, stride=ZP), :] = (v * phi[0, z])[:N] + acc[z] + recv_v[z]

    lane = lax.broadcasted_iota(jnp.int32, (ZP, L), 1)
    total = N * N
    for t in range(-(-total // L)):
        x, off = divmod(t * L, N)
        val = tb[x * ZP:(x + 1) * ZP, :]
        if off:
            val = pltpu.roll(val, L - off, 1)
        if x + 1 < N:
            more = pltpu.roll(tb[(x + 1) * ZP:(x + 2) * ZP, :], N - off, 1)
            val = jnp.where(lane < N - off, val, more)
        width = min(L, total - t * L)
        out[:, 0, t * L:t * L + width] = val[:ZL, :width]

    def left1(d, c):
        b = lax.rem(band + d, NBAND)
        copy(send1.at[b], recv1.at[b], s1.at[b], r1.at[b], b, fft).wait_send()
        return c

    lax.fori_loop(1, NBAND, left1, 0)

    def left2(d, c):
        f = lax.rem(fft + d, NF)
        copy(cols, all_cols.at[f], sk.at[f], rk.at[f], band, f).wait_send()
        stick_block(0, d, band, f).wait_send()
        for k in range(4 * PARTS - 3, 4 * PARTS):
            part(k, f).wait_send()
        return c

    lax.fori_loop(1, NF, left2, 0)

    def left2n(f, c):
        stick_block(1, f, prv, f).wait_send()
        return c

    lax.fori_loop(0, NF, left2n, 0)
    to_next(0, ZL).wait_send()
    for first, count, hop in ROUTES:
        if hop:
            @pl.when(lax.rem(band, 16) == 2 * hop)
            def _():
                from_relay(first, count).wait_send()


def local(coefficients, owned_sticks, stick_counts, stick_columns, band_order):
    tables = jnp.asarray(cas_parts())
    vmem = pl.BlockSpec(memory_space=pltpu.VMEM)
    dma = pltpu.SemaphoreType.DMA
    out = pl.pallas_call(
        kernel,
        out_shape=jax.ShapeDtypeStruct((ZL, 1, N * N), F32),
        in_specs=[pl.BlockSpec(memory_space=pltpu.HBM)] * 6,
        out_specs=vmem,
        scratch_shapes=[
            pltpu.VMEM((NBAND, CAP * N), F32),
            pltpu.VMEM((1, NBAND * CAP), jnp.int32),
            pltpu.VMEM((1, STICKS), jnp.int32),
            pltpu.VMEM((1, STICKS), jnp.int32),
            pltpu.SMEM((NBAND,), jnp.int32),
            pltpu.VMEM((7 * L, 2 * L), BF16),
            pltpu.VMEM((NBAND * CAPP, L), F32),
            pltpu.VMEM((NBAND, CAPP, L), F32),
            pltpu.VMEM((NBAND, CAP, L), F32),
            pltpu.VMEM((NBAND, CAP, L), F32),
            pltpu.VMEM((STICKS, NBAND * CAPP), BF16),
            pltpu.VMEM((STICKS, L), F32),
            pltpu.VMEM((1, NBAND * CAPP), jnp.int32),
            pltpu.VMEM((8, STP), F32),
            pltpu.VMEM((NF, 1, STICKS), jnp.int32),
            pltpu.VMEM((NF, 1, STP), F32),
            pltpu.VMEM((NF, STP, 2 * L), BF16),
            pltpu.VMEM((NF, ZP, STP), F32),
            pltpu.VMEM((2, NF, ZP, STP), F32),
            pltpu.VMEM((2, ZL, L, L), F32),
            pltpu.VMEM((L * ZP, L), F32),
            pltpu.VMEM((L * ZP, L), F32),
            pltpu.VMEM((ZL, L, L), F32),
            pltpu.VMEM((2, NF, ZL, ZP, L), F32),
            pltpu.VMEM((2, NF, ZL, ZP, L), F32),
            pltpu.VMEM((2, NF, ZL, ZP, L), F32),
            pltpu.VMEM((2, NF, ZL, ZP, L), F32),
            pltpu.VMEM((ZL, N, L), F32),
            pltpu.VMEM((ZL, N, L), F32),
            pltpu.VMEM((ZL, N, L), F32),
            pltpu.VMEM((4, N, L), F32),
            dma((NF,)), dma((NF,)),
            dma((NBAND,)), dma((NBAND,)),
            dma((2, NF)), dma((2, NF)),
            dma((4 * PARTS, NF)), dma((2 * PARTS, NF)), dma((2 * PARTS, NF)),
            dma, dma, dma, dma,
            dma((6,)),
        ],
        compiler_params=pltpu.CompilerParams(
            collective_id=0, has_side_effects=True, vmem_limit_bytes=48 * 1024 * 1024),
    )(*[pltpu.with_memory_space_constraint(a, pltpu.HBM) for a in (
        coefficients, owned_sticks, stick_counts, stick_columns, band_order, tables)])
    return out.reshape(1, ZL, N * N)


def solution(mesh):
    placed = (P(None, ("band", "fft")), P("fft", None), P("fft", None), P("fft", None), P())
    return jax.shard_map(
        local, mesh=mesh, in_specs=placed, out_specs=P("band", "fft", None), check_vma=False
    )
```
